512 devices in a mesh: fsdp: 16 (over z_lo, x, core), space: 32 (over y, z_hi).
Axes of the slice: x: 4, y: 8, z: 8 (z_hi: 4, z_lo: 2; z = z_hi * 2 + z_lo), core: 2. Of those that a mesh axis runs over, the one named last changes fastest.
Arguments:
- features: bfloat16 [16, 32, 96, 512], P('fsdp', 'space'), may hold values from -6 to 6
- w_first: bfloat16 [96, 2592], P('fsdp'), may hold values from -0.125 to 0.125
- w_second: bfloat16 [96, 2592], P('fsdp'), may hold values from -0.125 to 0.125
- neighbours: int32 [16, 32, 6], P('fsdp', 'space'), may hold values from -1 to 0, as said below
- live_counts: int32 [16, 32], P('fsdp', 'space'), may hold values from 1 to 1, as said below
- output_gradient: bfloat16 [16, 32, 96, 512], P('fsdp', 'space'), may hold values from -6 to 6
Outputs:
- block_out: bfloat16 [16, 32, 96, 512], P('fsdp', 'space')
- grad_in: bfloat16 [16, 32, 96, 512], P('fsdp', 'space')
- grad_first: float32 [96, 2592], P('fsdp')
- grad_second: float32 [96, 2592], P('fsdp')
The draws below stay inside these ranges and needn't reach their ends.
Inputs may be any that keep to these rules, and one draw needn't show every extreme that they name: `live_counts`: the occupied slots of a device are its first ones; in every scene some device has all 1 slots occupied. Blocks lie on a lattice, device d holding the blocks of one layer along x: the relation is symmetric (if neighbours[s, f] names block r then neighbours[r, f ^ 1] names s), only occupied slots name or are named, and device 0 has none across face 0, device 32 - 1 none across face 1.
All inputs are finite; a program needn't handle non-finite values.
Results may differ from the reference program's by a relative error of at most 0.0054.
Values may be sent and summed in bfloat16 or wider, within the bound.
A program may use at most 64 MiB of HBM per device.

```python
import jax
import jax.numpy as jnp
from jax import lax

CHANNEL_COUNT = 96
BLOCK_EDGE = 8
BMAX = 1
SCENE_COUNT = 16
SLOT_COUNT = 32
N_FSDP = 16
N_SPACE = 32


def locate(want_row, want_col, have_row, have_col, active_present):
    matches = (want_row[:, :, None] == have_row[:, None, :]) & (want_col[:, :, None] == have_col[:, None, :]) & active_present[:, None, :]
    slot_ids = jnp.arange(want_row.shape[1], dtype=jnp.int32)[None, None, :]
    return jnp.sum(jnp.where(matches, slot_ids + 1, 0), axis=2) - 1


def scene_layout(scene_key):
    key_count, key_full, key_place = jax.random.split(scene_key, 3)
    counts = jax.random.randint(key_count, (N_SPACE,), 1, BMAX + 1)
    fullest = jax.random.randint(key_full, (), 0, N_SPACE)
    counts = jnp.where(jnp.arange(N_SPACE) == fullest, BMAX, counts).astype(jnp.int32)
    place_keys = jax.random.split(key_place, N_SPACE)
    places = jax.vmap(lambda one_key: jax.random.permutation(one_key, 2 * BMAX))(place_keys)[:, :BMAX]
    active = jnp.arange(BMAX)[None, :] < counts[:, None]
    row_pos = places // BMAX
    col_pos = places % BMAX
    lower_row = jnp.concatenate([row_pos[:1], row_pos[:-1]], axis=0)
    lower_col = jnp.concatenate([col_pos[:1], col_pos[:-1]], axis=0)
    lower_active = jnp.concatenate([jnp.zeros_like(active[:1]), active[:-1]], axis=0)
    upper_row = jnp.concatenate([row_pos[1:], row_pos[-1:]], axis=0)
    upper_col = jnp.concatenate([col_pos[1:], col_pos[-1:]], axis=0)
    upper_active = jnp.concatenate([active[1:], jnp.zeros_like(active[:1])], axis=0)
    found = [locate(row_pos, col_pos, lower_row, lower_col, lower_active), locate(row_pos, col_pos, upper_row, upper_col, upper_active), locate(row_pos - 1, col_pos, row_pos, col_pos, active), locate(row_pos + 1, col_pos, row_pos, col_pos, active), locate(row_pos, col_pos - 1, row_pos, col_pos, active), locate(row_pos, col_pos + 1, row_pos, col_pos, active)]
    stacked = jnp.stack(found, axis=2)
    stacked = jnp.where(active[:, :, None], stacked, -1).astype(jnp.int32)
    return (counts, stacked.reshape(N_SPACE * BMAX, 6))


def layout(base_key):
    scene_keys = jax.vmap(lambda index_value: jax.random.fold_in(base_key, index_value))(jnp.arange(N_FSDP))
    return jax.vmap(scene_layout)(scene_keys)


def draw_neighbours(key, part):
    return layout(jax.random.fold_in(key, 11))[1]


def draw_live_counts(key, part):
    return layout(jax.random.fold_in(key, 11))[0]


def shard_levels(stream_key, extent, cuts, low, high):
    gain = 1.0
    for dim, blocks in cuts:
        draws = jax.random.uniform(jax.random.fold_in(jax.random.fold_in(stream_key, 6), dim), (blocks,), jnp.float32, low / len(cuts), high / len(cuts))
        gain = gain * jnp.repeat(jnp.exp(draws), extent[dim] // blocks).reshape((-1,) + (1,) * (len(extent) - 1 - dim))
    return gain


def centred(own_key, dims, scale, most, pieces=(), kind=jnp.bfloat16):
    loudness = shard_levels(own_key, dims, pieces, -0.22, 0.18) if pieces else 1.0
    array = jax.random.normal(own_key, dims, jnp.float32) * scale * loudness
    return jnp.minimum(jnp.maximum(array, -most), most).astype(kind)


def setup_inputs(seed: int = 0) -> dict:
    seeds = jax.random.split(jax.random.key(seed), 7)
    features = centred(seeds[0], (SCENE_COUNT, SLOT_COUNT, CHANNEL_COUNT, BLOCK_EDGE**3), 1.0, 6.0, ((0, 16), (1, 32)))
    w_first = centred(seeds[1], (CHANNEL_COUNT, 27 * CHANNEL_COUNT), (27 * CHANNEL_COUNT) ** -0.5, 0.125, ((0, 16),))
    w_second = centred(seeds[2], (CHANNEL_COUNT, 27 * CHANNEL_COUNT), (27 * CHANNEL_COUNT) ** -0.5, 0.125, ((0, 16),))
    neighbours = draw_neighbours(jax.random.fold_in(seeds[6], 71), 0)
    live_counts = draw_live_counts(jax.random.fold_in(seeds[6], 71), 0)
    output_gradient = centred(seeds[5], (SCENE_COUNT, SLOT_COUNT, CHANNEL_COUNT, BLOCK_EDGE**3), 1.0, 6.0, ((0, 16), (1, 32)))
    return {"features": features, "w_first": w_first, "w_second": w_second, "neighbours": neighbours, "live_counts": live_counts, "output_gradient": output_gradient}


epsilon = 1e-05

def normalize_act(values):
    centre = lax.optimization_barrier(jnp.mean(values, axis=1, keepdims=True))
    spread = lax.optimization_barrier(jnp.mean(jnp.square(values - centre), axis=1, keepdims=True))
    return jax.nn.silu((values - centre) * lax.rsqrt(spread + epsilon))

def layer_of(blocks, which_face):
    axis_pos = 2 + which_face // 2
    index_pos = 0 if which_face % 2 == 0 else blocks.shape[axis_pos] - 1
    return lax.index_in_dim(blocks, index_pos, axis_pos, keepdims=False)

def with_margins(blocks, pulled):
    edge_len = blocks.shape[2]
    padded = jnp.pad(blocks, ((0, 0), (0, 0), (1, 1), (1, 1), (1, 1)))
    middle = slice(1, edge_len + 1)
    padded = padded.at[:, :, 0, middle, middle].set(pulled[0])
    padded = padded.at[:, :, edge_len + 1, middle, middle].set(pulled[1])
    padded = padded.at[:, :, middle, 0, middle].set(pulled[2])
    padded = padded.at[:, :, middle, edge_len + 1, middle].set(pulled[3])
    padded = padded.at[:, :, middle, middle, 0].set(pulled[4])
    padded = padded.at[:, :, middle, middle, edge_len + 1].set(pulled[5])
    return padded

def unfold(padded, edge_len):
    columns = []
    for shift_x in range(3):
        for shift_y in range(3):
            for shift_z in range(3):
                columns.append(padded[:, :, shift_x:shift_x + edge_len, shift_y:shift_y + edge_len, shift_z:shift_z + edge_len])
    stacked = jnp.stack(columns, axis=1)
    return stacked.reshape(padded.shape[0], 27 * padded.shape[1], edge_len ** 3)

def flipped(weight):
    channels = weight.shape[0]
    tap_major = weight.reshape(channels, 27, channels)[:, ::-1, :]
    return jnp.transpose(tap_major, (2, 1, 0)).reshape(channels, 27 * channels)

def neighbour_faces(blocks, near_slots, device_of):
    slot_total = blocks.shape[0]
    layers_flat = [layer_of(blocks, which_face).reshape(slot_total, -1) for which_face in range(6)]
    offsets = [-1, 1, 0, 0, 0, 0]
    pulled = []
    for which_face in range(6):
        source = layers_flat[which_face ^ 1]
        wanted = near_slots[:, which_face]
        target = (device_of + offsets[which_face]) * BMAX + wanted
        target = jnp.clip(target, 0, slot_total - 1).astype(jnp.int32)
        fetched = jnp.take(source, target, axis=0)
        fetched = jnp.where((wanted >= 0)[:, None], fetched, jnp.zeros_like(fetched))
        pulled.append(fetched.reshape(slot_total, blocks.shape[1], BLOCK_EDGE, BLOCK_EDGE))
    return pulled

def convolve(weight, flat_blocks, near_slots, device_of):
    slot_total, channels = (flat_blocks.shape[0], flat_blocks.shape[1])
    cube_blocks = flat_blocks.reshape(slot_total, channels, BLOCK_EDGE, BLOCK_EDGE, BLOCK_EDGE)
    padded = with_margins(cube_blocks, neighbour_faces(cube_blocks, near_slots, device_of))

    def single(block_pad):
        return jnp.dot(weight, unfold(block_pad[None], BLOCK_EDGE)[0], preferred_element_type=jnp.float32)
    return (lax.map(single, padded), padded)

def weight_term(grads, padded):
    channels = grads.shape[1]

    def accumulate(running, item_pair):
        grad_block, block_pad = item_pair
        columns = unfold(block_pad[None], BLOCK_EDGE)[0]
        return (running + jnp.dot(grad_block, columns.T, preferred_element_type=jnp.float32), None)
    running, discarded_result = lax.scan(accumulate, jnp.zeros((channels, 27 * channels), jnp.float32), (grads, padded))
    return running

def reference(features, w_first, w_second, neighbours, live_counts, output_gradient):
    slot_total = features.shape[1]
    device_of = (jnp.arange(slot_total) // BMAX).astype(jnp.int32)
    local_slot = (jnp.arange(slot_total) % BMAX).astype(jnp.int32)
    flip_one = flipped(w_first)
    mirrored_second = flipped(w_second)

    def scene(inputs):
        blocks_in, near_slots, live_row, grad_top = inputs
        occupied = (local_slot < live_row[device_of]).astype(jnp.float32)[:, None, None]
        inputs_f32 = blocks_in.astype(jnp.float32)
        act_first, pull_first = jax.vjp(normalize_act, inputs_f32)
        active_one = (act_first * occupied).astype(jnp.bfloat16)
        hidden, pad_one = convolve(w_first, active_one, near_slots, device_of)
        act_second, pull_second = jax.vjp(normalize_act, hidden)
        active_two = (act_second * occupied).astype(jnp.bfloat16)
        branch_out, pad_two = convolve(w_second, active_two, near_slots, device_of)
        block_out = ((inputs_f32 + branch_out) * occupied).astype(jnp.bfloat16)
        grad_two = (grad_top.astype(jnp.float32) * occupied).astype(jnp.bfloat16)
        term_two = weight_term(grad_two, pad_two)
        back_two = convolve(mirrored_second, grad_two, near_slots, device_of)[0]
        grad_hidden = pull_second(back_two * occupied)[0]
        grad_one = (grad_hidden * occupied).astype(jnp.bfloat16)
        term_one = weight_term(grad_one, pad_one)
        back_one = convolve(flip_one, grad_one, near_slots, device_of)[0]
        grad_input = pull_first(back_one * occupied)[0]
        grad_in = ((grad_top.astype(jnp.float32) + grad_input) * occupied).astype(jnp.bfloat16)
        return (block_out, grad_in, term_one, term_two)
    results = lax.map(scene, (features, neighbours, live_counts, output_gradient))
    return (results[0], results[1], lax.optimization_barrier(jnp.sum(results[2], axis=0)), lax.optimization_barrier(jnp.sum(results[3], axis=0)))
```

```python
import jax
import jax.numpy as jnp
from jax import lax
from jax.experimental import pallas as pl
from jax.experimental.pallas import tpu as pltpu
from jax.sharding import PartitionSpec as P

MESH = pl.DeviceIdType.MESH
F32 = jnp.float32
BF16 = jnp.bfloat16

CH = 96
LT = 128
KA = 9 * CH
KP = 896
HALF = 11 * LT
EPS = 1e-05


def xor(value, pattern):
    for bit in (1, 2, 4):
        if pattern & bit:
            value = value + (1 - 2 * lax.rem(lax.div(value, bit), 2)) * bit
    return value


def half_turn(tile):
    return pltpu.roll(tile, 64, 1)


def paired(tiles, low):
    t0, t1, t2, t3 = tiles
    return (
        jnp.where(low, t0, half_turn(t2)),
        jnp.where(low, half_turn(t0), t2),
        jnp.where(low, t1, half_turn(t3)),
        jnp.where(low, half_turn(t1), t3),
    )


def unpaired(tiles, low):
    p0, p1, p2, p3 = tiles
    return (
        jnp.where(low, p0, half_turn(p1)),
        jnp.where(low, p2, half_turn(p3)),
        jnp.where(low, half_turn(p0), p1),
        jnp.where(low, half_turn(p2), p3),
    )


def normalized(u):
    centred = u - jnp.mean(u, axis=0, keepdims=True)
    scale = lax.rsqrt(jnp.mean(centred * centred, axis=0, keepdims=True) + EPS)
    return centred * scale, scale


def sigmoid(v):
    return 1.0 / (1.0 + jnp.exp(-v))


def act_vjp(norm, scale, cotangent):
    gate = sigmoid(norm)
    inner = cotangent * (gate * (1.0 + norm * (1.0 - gate)))
    return scale * (
        inner
        - jnp.mean(inner, axis=0, keepdims=True)
        - norm * jnp.mean(inner * norm, axis=0, keepdims=True)
    )


def kernel(
    feat_ref, wone_ref, wtwo_ref, near_ref, live_ref, grad_ref,
    bout_ref, gin_ref, gone_ref, gtwo_ref,
    w_buf, w_full, w_flip, halo_out, halo_in, cols, x_buf, n_buf, r_buf, gp_buf,
    term, one_out, one_in, two_out, two_in, sum_src, sum_in, piece, piece_in, whole,
    w_send, w_recv, f_send, f_recv, halo_send, halo_recv,
    one_send, one_recv, two_send, two_recv, y_send, y_recv, z_send, z_recv, g_send, g_recv,
):
    fsdp = lax.axis_index("fsdp")
    space = lax.axis_index("space")
    chip, core = lax.div(fsdp, 2), lax.rem(fsdp, 2)
    row, col = lax.div(space, 4), lax.rem(space, 4)
    sibling = {"fsdp": chip * 2 + (1 - core), "space": space}

    def chip_mate(j):
        return {"fsdp": xor(chip, j) * 2 + core, "space": space}

    def row_mate(j):
        return {"fsdp": fsdp, "space": xor(row, j) * 4 + col}

    def col_mate(j):
        return {"fsdp": fsdp, "space": row * 4 + xor(col, j)}

    below = {"fsdp": fsdp, "space": lax.rem(space + 31, 32)}
    above = {"fsdp": fsdp, "space": lax.rem(space + 1, 32)}

    mates = (
        [sibling, below, above]
        + [chip_mate(j) for j in range(1, 8)]
        + [row_mate(j) for j in range(1, 8)]
        + [col_mate(j) for j in range(1, 4)]
    )
    barrier = pltpu.get_barrier_semaphore()
    for mate in mates:
        pl.semaphore_signal(barrier, inc=1, device_id=mate, device_id_type=MESH)

    sent = []

    def send(src, dst, send_sem, recv_sem, device):
        copy = pltpu.make_async_remote_copy(
            src_ref=src, dst_ref=dst, send_sem=send_sem, recv_sem=recv_sem,
            device_id=device, device_id_type=MESH,
        )
        copy.start()
        sent.append(copy)
        return copy

    for k, ref in enumerate((wone_ref, wtwo_ref)):
        rows = ref[...].astype(F32)
        gap = jnp.zeros((6, KP - KA), F32)
        parts = []
        for a in range(3):
            parts += [rows[:, a * KA : (a + 1) * KA], gap]
        flat = jnp.concatenate(parts + [jnp.zeros((6, LT), F32)], axis=1)
        flat = jnp.concatenate([flat, jnp.zeros((2, 2 * HALF), F32)], axis=0)
        w_buf[k, 0] = jnp.concatenate([flat[:, :HALF], flat[:, HALF:]], axis=0).astype(BF16)

    pl.semaphore_wait(barrier, len(mates))

    w_copy, f_copy = [], []
    for k in range(2):
        own = [send(w_buf.at[k, 0], w_buf.at[k, 8], f_send.at[k, 0], f_recv.at[k, 0], sibling)]
        f_copy.append(own)
        w_copy.append([
            send(w_buf.at[k, 0], w_buf.at[k, j], w_send.at[k, j - 1], w_recv.at[k, j - 1], chip_mate(j))
            for j in range(1, 8)
        ])

    def forward_weight(k):
        for j in range(1, 8):
            w_copy[k][j - 1].wait_recv()
            f_copy[k].append(
                send(w_buf.at[k, j], w_buf.at[k, 8 + j], f_send.at[k, j], f_recv.at[k, j], sibling)
            )

    lane = lax.broadcasted_iota(jnp.int32, (1, LT), 1)
    z_pos, y_pos = lane & 7, (lane >> 3) & 7
    low = lane < 64

    def flag(cond):
        return jnp.where(cond, 1.0, 0.0).astype(F32)

    def named(face):
        return jnp.where(near_ref[0, 0, face] >= 0, 1.0, 0.0).astype(F32)

    occupied = jnp.where(live_ref[0, 0] > 0, 1.0, 0.0).astype(F32)
    low_f, high_f = flag(low), flag(lane >= 64)
    in_z = {c: flag((z_pos + c - 1 >= 0) & (z_pos + c - 1 < 8)) for c in (0, 2)}
    in_y = {b: flag((y_pos + b - 1 >= 0) & (y_pos + b - 1 < 8)) for b in (0, 2)}

    def wide(mask):
        return jnp.broadcast_to(mask, (CH, LT)).astype(BF16)

    inside = {"low": high_f, "mid": jnp.ones((1, LT), F32), "high": low_f}
    z_keep = {c: wide(in_z[c]) for c in (0, 2)}
    y_keep = {b: wide(in_y[b]) for b in (0, 2)}
    z_wrap = {
        (c, w): wide((1.0 - in_z[c]) * named(4 + c // 2) * inside[w]) for c in (0, 2) for w in inside
    }
    y_wrap = {}
    for b in (0, 2):
        for w in inside:
            base = (1.0 - in_y[b]) * named(2 + b // 2) * inside[w]
            for c in range(3):
                y_wrap[b, c, w] = wide(base if c == 1 else base * in_z[c])

    def unroll_tile(which, j, tile):
        w = "low" if j == 0 else "high" if j == 5 else "mid"
        for c in range(3):
            if c == 1:
                along = tile
            else:
                dz = c - 1
                along = (
                    pltpu.roll(tile, -dz % LT, 1) * z_keep[c]
                    + pltpu.roll(tile, 7 * dz % LT, 1) * z_wrap[c, w]
                )
            for b in range(3):
                if b == 1:
                    both = along
                else:
                    dy = b - 1
                    both = (
                        pltpu.roll(along, -8 * dy % LT, 1) * y_keep[b]
                        + pltpu.roll(along, 56 * dy % LT, 1) * y_wrap[b, c, w]
                    )
                tap = b * 3 + c
                cols[which, tap * CH : (tap + 1) * CH, j * LT : (j + 1) * LT] = both

    halo_copy = {}

    def send_halo(which, first, last):
        halo_out[which, 0] = half_turn(first)
        halo_out[which, 1] = half_turn(last)
        halo_copy[which] = [
            send(halo_out.at[which, 0], halo_in.at[which, 0], halo_send.at[which, 0],
                 halo_recv.at[which, 0], below),
            send(halo_out.at[which, 1], halo_in.at[which, 1], halo_send.at[which, 1],
                 halo_recv.at[which, 1], above),
        ]

    def unroll_middle(which, tiles):
        cols[which, KA:KP, :] = jnp.zeros((KP - KA, 6 * LT), BF16)
        for j in range(4):
            unroll_tile(which, j + 1, tiles[j])

    def unroll_edges(which):
        for copy in halo_copy[which]:
            copy.wait_recv()
        lower = halo_out[which, 1] * wide(high_f) + halo_in[which, 1] * wide(low_f * named(0))
        unroll_tile(which, 0, lower)
        upper = halo_out[which, 0] * wide(low_f) + halo_in[which, 0] * wide(high_f * named(1))
        unroll_tile(which, 5, upper)

    def lanes_of(array, j):
        return array[:, j * LT : (j + 1) * LT]

    x_tiles = paired([feat_ref[0, 0, :, j * LT : (j + 1) * LT].astype(F32) for j in range(4)], low)
    a_one = []
    for j in range(4):
        norm, scale = normalized(x_tiles[j])
        x_buf[0, j] = x_tiles[j]
        n_buf[0, j], r_buf[0, j] = norm, scale
        a_one.append((occupied * (norm * sigmoid(norm))).astype(BF16))
    send_halo(0, a_one[0], a_one[3])
    g_tiles = paired([grad_ref[0, 0, :, j * LT : (j + 1) * LT].astype(F32) for j in range(4)], low)
    g_two = []
    for j in range(4):
        x_buf[1, j] = g_tiles[j]
        g_two.append((occupied * g_tiles[j]).astype(BF16))
    send_halo(1, g_two[0], g_two[3])
    unroll_middle(0, a_one)
    unroll_middle(1, g_two)

    r_row = lax.broadcasted_iota(jnp.int32, (LT, CH), 0)
    r_col = lax.broadcasted_iota(jnp.int32, (LT, CH), 1)
    r_core = core + (r_row >> 6) * (1 - 2 * core)
    r_owner = (((r_row >> 3) & 7) ^ chip) * 2 + r_core
    spread = jnp.where(((r_row & 7) < 6) & (r_owner * 6 + (r_row & 7) == r_col), 1.0, 0.0).astype(BF16)

    def spread_rows(tiles):
        whole_g = jnp.concatenate(list(tiles), axis=1)
        return jnp.dot(spread, whole_g, preferred_element_type=F32).astype(BF16)

    gp_buf[1] = spread_rows(g_two)

    p_row = lax.broadcasted_iota(jnp.int32, (2 * CH, 256), 0)
    p_col = lax.broadcasted_iota(jnp.int32, (2 * CH, 256), 1)
    p_half = jnp.where(p_row >= CH, 1, 0)
    p_out = p_row - CH * p_half
    p_owner = (p_out * 43691) >> 18
    p_slot = ((p_owner >> 1) ^ chip) + 8 * ((p_owner & 1) ^ core)
    pick = jnp.where(p_slot * 16 + p_half * 8 + (p_out - 6 * p_owner) == p_col, 1.0, 0.0).astype(BF16)

    def assemble(k):
        for copy in f_copy[k]:
            copy.wait_recv()
        packed = w_buf[k].reshape(256, HALF)
        both = jnp.dot(pick, packed, preferred_element_type=F32).astype(BF16)
        w_full[k, :, :HALF] = both[:CH]
        w_full[k, :, HALF:] = both[CH:]

    def flip(k):
        for a in range(3):
            turned = jnp.transpose(w_full[k, :, (2 - a) * KP : (3 - a) * KP])
            blocks = [turned[(8 - t) * CH : (9 - t) * CH, :] for t in range(9)]
            w_flip[k, :, a * KP : (a + 1) * KP] = jnp.concatenate(
                blocks + [jnp.zeros((CH, KP - KA), BF16)], axis=1
            )

    def convolve(weights, k, which):
        total = None
        for a in range(3):
            part = jnp.dot(
                weights[k, :, a * KP : (a + 1) * KP],
                cols[which, :, a * LT : a * LT + 512],
                preferred_element_type=F32,
            )
            total = part if total is None else total + part
        return total

    one_copy, two_copy, y_copy, z_copy, g_copy = {}, {}, {}, {}, {}

    def start_term(m, which):
        term[m, :, 3 * KP :] = jnp.zeros((64, LT), F32)
        one_copy[m] = []
        for a in range(3):
            part = lax.dot_general(
                gp_buf[m], cols[which, :, a * LT : a * LT + 512],
                (((1,), (1,)), ((), ())), preferred_element_type=F32,
            )
            one_out[m, a] = part[64:].astype(BF16)
            one_copy[m].append(
                send(one_out.at[m, a], one_in.at[m, a], one_send.at[m, a], one_recv.at[m, a], sibling)
            )
            term[m, :, a * KP : (a + 1) * KP] = part[:64]

    def reduce_chips(m):
        for a in range(3):
            one_copy[m][a].wait_recv()
            term[m, :, a * KP : (a + 1) * KP] += one_in[m, a].astype(F32)
        two_copy[m] = []
        for j in range(1, 8):
            two_out[m, j - 1] = jnp.concatenate(
                [term[m, 8 * j : 8 * j + 8, :HALF], term[m, 8 * j : 8 * j + 8, HALF:]], axis=0
            ).astype(BF16)
            two_copy[m].append(
                send(two_out.at[m, j - 1], two_in.at[m, j - 1], two_send.at[m, j - 1],
                     two_recv.at[m, j - 1], chip_mate(j))
            )

    def reduce_rows(m):
        total = jnp.concatenate([term[m, :8, :HALF], term[m, :8, HALF:]], axis=0)
        for j in range(1, 8):
            two_copy[m][j - 1].wait_recv()
            total = total + two_in[m, j - 1].astype(F32)
        tiles = [total[:8, n * LT : (n + 1) * LT] for n in range(11)]
        tiles += [total[8:, n * LT : (n + 1) * LT] for n in range(10)]
        for p in range(7):
            sum_src[m, p] = jnp.concatenate(tiles[3 * p : 3 * p + 3], axis=1)
        sum_src[m, 7] = jnp.zeros((8, 3 * LT), F32)
        y_copy[m] = [
            send(sum_src.at[m, xor(row, j)], sum_in.at[m, j - 1], y_send.at[m, j - 1],
                 y_recv.at[m, j - 1], row_mate(j))
            for j in range(1, 8)
        ]

    def reduce_cols(m):
        total = sum_src[m, row]
        for j in range(1, 8):
            y_copy[m][j - 1].wait_recv()
            total = total + sum_in[m, j - 1]
        piece[m] = total
        z_copy[m] = [
            send(piece.at[m], piece_in.at[m, j - 1], z_send.at[m, j - 1], z_recv.at[m, j - 1], col_mate(j))
            for j in range(1, 4)
        ]

    def share_rows(m):
        for copy in z_copy[m]:
            copy.wait_recv()
        whole[m, row] = (piece[m] + piece_in[m, 0]) + (piece_in[m, 1] + piece_in[m, 2])
        g_copy[m] = [
            send(whole.at[m, row], whole.at[m, row], g_send.at[m, j - 1], g_recv.at[m, j - 1], row_mate(j))
            for j in range(1, 8)
        ]

    def finish(m, out_ref):
        for copy in g_copy[m]:
            copy.wait_recv()
        flat = jnp.concatenate([whole[m, p][:6] for p in range(7)], axis=1)
        out_ref[...] = jnp.concatenate([flat[:, a * KP : a * KP + KA] for a in range(3)], axis=1)

    forward_weight(0)
    unroll_edges(0)
    unroll_edges(1)
    assemble(0)
    hidden = convolve(w_full, 0, 0)
    a_two = []
    for j in range(4):
        norm, scale = normalized(lanes_of(hidden, j))
        n_buf[1, j], r_buf[1, j] = norm, scale
        a_two.append((occupied * (norm * sigmoid(norm))).astype(BF16))
    send_halo(2, a_two[0], a_two[3])
    forward_weight(1)
    unroll_middle(2, a_two)
    unroll_edges(2)

    start_term(1, 2)

    assemble(1)
    flip(1)
    back = convolve(w_flip, 1, 1)
    g_one = []
    for j in range(4):
        inner = act_vjp(n_buf[1, j], r_buf[1, j], occupied * lanes_of(back, j))
        g_one.append((occupied * inner).astype(BF16))
    send_halo(3, g_one[0], g_one[3])
    gp_buf[0] = spread_rows(g_one)
    reduce_chips(1)
    start_term(0, 0)

    unroll_middle(3, g_one)
    branch = convolve(w_full, 1, 2)
    reduce_chips(0)
    reduce_rows(1)
    outs = unpaired([occupied * (x_buf[0, j] + lanes_of(branch, j)) for j in range(4)], low)
    for j in range(4):
        bout_ref[0, 0, :, j * LT : (j + 1) * LT] = outs[j].astype(BF16)
    flip(0)
    reduce_cols(1)
    unroll_edges(3)
    reduce_rows(0)
    back = convolve(w_flip, 0, 3)
    share_rows(1)
    reduce_cols(0)
    outs = []
    for j in range(4):
        inner = act_vjp(n_buf[0, j], r_buf[0, j], occupied * lanes_of(back, j))
        outs.append(occupied * (x_buf[1, j] + inner))
    outs = unpaired(outs, low)
    for j in range(4):
        gin_ref[0, 0, :, j * LT : (j + 1) * LT] = outs[j].astype(BF16)
    share_rows(0)
    finish(1, gtwo_ref)
    finish(0, gone_ref)
    for copy in sent:
        copy.wait_send()


def body(features, w_first, w_second, neighbours, live_counts, output_gradient):
    vmem = pl.BlockSpec(memory_space=pltpu.VMEM)
    smem = pl.BlockSpec(memory_space=pltpu.SMEM)
    dma = pltpu.SemaphoreType.DMA
    return pl.pallas_call(
        kernel,
        out_shape=(
            jax.ShapeDtypeStruct(features.shape, BF16),
            jax.ShapeDtypeStruct(features.shape, BF16),
            jax.ShapeDtypeStruct(w_first.shape, F32),
            jax.ShapeDtypeStruct(w_second.shape, F32),
        ),
        in_specs=[vmem, vmem, vmem, smem, smem, vmem],
        out_specs=(vmem, vmem, vmem, vmem),
        scratch_shapes=[
            pltpu.VMEM((2, 16, 16, HALF), BF16),
            pltpu.VMEM((2, CH, 2 * HALF), BF16),
            pltpu.VMEM((2, CH, 3 * KP), BF16),
            pltpu.VMEM((4, 2, CH, LT), BF16),
            pltpu.VMEM((4, 2, CH, LT), BF16),
            pltpu.VMEM((4, KP, 6 * LT), BF16),
            pltpu.VMEM((2, 4, CH, LT), F32),
            pltpu.VMEM((2, 4, CH, LT), F32),
            pltpu.VMEM((2, 4, 1, LT), F32),
            pltpu.VMEM((2, LT, 512), BF16),
            pltpu.VMEM((2, 64, 2 * HALF), F32),
            pltpu.VMEM((2, 3, 64, KP), BF16),
            pltpu.VMEM((2, 3, 64, KP), BF16),
            pltpu.VMEM((2, 7, 16, HALF), BF16),
            pltpu.VMEM((2, 7, 16, HALF), BF16),
            pltpu.VMEM((2, 8, 8, 3 * LT), F32),
            pltpu.VMEM((2, 7, 8, 3 * LT), F32),
            pltpu.VMEM((2, 8, 3 * LT), F32),
            pltpu.VMEM((2, 3, 8, 3 * LT), F32),
            pltpu.VMEM((2, 8, 8, 3 * LT), F32),
            dma((2, 7)), dma((2, 7)), dma((2, 8)), dma((2, 8)), dma((4, 2)), dma((4, 2)),
            dma((2, 3)), dma((2, 3)), dma((2, 7)), dma((2, 7)), dma((2, 7)), dma((2, 7)),
            dma((2, 3)), dma((2, 3)), dma((2, 7)), dma((2, 7)),
        ],
        compiler_params=pltpu.CompilerParams(
            collective_id=0, has_side_effects=True, vmem_limit_bytes=48 * 1024 * 1024
        ),
    )(features, w_first, w_second, neighbours, live_counts, output_gradient)


def solution(mesh):
    blocks = P("fsdp", "space", None, None)
    weights = P("fsdp", None)
    return jax.shard_map(
        body,
        mesh=mesh,
        in_specs=(blocks, weights, weights, P("fsdp", "space", None), P("fsdp", "space"), blocks),
        out_specs=(blocks, blocks, weights, weights),
        check_vma=False,
    )
```

```python
import jax
import jax.numpy as jnp
from jax import lax
from jax.experimental import pallas as pl
from jax.experimental.pallas import tpu as pltpu
from jax.sharding import PartitionSpec as P

MESH = pl.DeviceIdType.MESH
F32 = jnp.float32
BF16 = jnp.bfloat16

CH = 96
LT = 128
KA = 9 * CH
KP = 896
HALF = 11 * LT
EPS = 1e-05
FAR_FIRST = (6, 2, 7, 5, 3, 1, 4)


def xor(value, pattern):
    for bit in (1, 2, 4):
        if pattern & bit:
            value = value + (1 - 2 * lax.rem(lax.div(value, bit), 2)) * bit
    return value


def half_turn(tile):
    return pltpu.roll(tile, 64, 1)


def paired(tiles, low):
    t0, t1, t2, t3 = tiles
    return (
        jnp.where(low, t0, half_turn(t2)),
        jnp.where(low, half_turn(t0), t2),
        jnp.where(low, t1, half_turn(t3)),
        jnp.where(low, half_turn(t1), t3),
    )


def unpaired(tiles, low):
    p0, p1, p2, p3 = tiles
    return (
        jnp.where(low, p0, half_turn(p1)),
        jnp.where(low, p2, half_turn(p3)),
        jnp.where(low, half_turn(p0), p1),
        jnp.where(low, half_turn(p2), p3),
    )


def normalized(u):
    centred = u - jnp.mean(u, axis=0, keepdims=True)
    scale = lax.rsqrt(jnp.mean(centred * centred, axis=0, keepdims=True) + EPS)
    return centred * scale, scale


def sigmoid(v):
    return 1.0 / (1.0 + jnp.exp(-v))


def act_vjp(norm, scale, cotangent):
    gate = sigmoid(norm)
    inner = cotangent * (gate * (1.0 + norm * (1.0 - gate)))
    return scale * (
        inner
        - jnp.mean(inner, axis=0, keepdims=True)
        - norm * jnp.mean(inner * norm, axis=0, keepdims=True)
    )


def kernel(
    feat_hbm, wone_hbm, wtwo_hbm, near_hbm, live_hbm, grad_hbm,
    bout_hbm, gin_hbm, gone_hbm, gtwo_hbm,
    bout_ref, gin_ref, gone_ref, gtwo_ref, feat_ref, wone_ref, wtwo_ref, near_ref, live_ref, grad_ref, load_sem, save_sem,
    w_buf, w_full, w_flip, halo_out, halo_in, cols, x_buf, n_buf, r_buf, gp_buf,
    term, one_out, one_in, two_out, two_in, sum_src, sum_in, piece, piece_in, whole,
    w_send, w_recv, f_send, f_recv, halo_send, halo_recv,
    one_send, one_recv, two_send, two_recv, y_send, y_recv, z_send, z_recv, g_send, g_recv,
):
    loads = [
        pltpu.make_async_copy(src, dst, load_sem.at[i])
        for i, (src, dst) in enumerate((
            (wone_hbm, wone_ref), (wtwo_hbm, wtwo_ref), (feat_hbm, feat_ref),
            (near_hbm, near_ref), (live_hbm, live_ref), (grad_hbm, grad_ref),
        ))
    ]
    for copy in loads:
        copy.start()
    fsdp = lax.axis_index("fsdp")
    space = lax.axis_index("space")
    chip, core = lax.div(fsdp, 2), lax.rem(fsdp, 2)
    row, col = lax.div(space, 4), lax.rem(space, 4)
    sibling = {"fsdp": chip * 2 + (1 - core), "space": space}

    def chip_mate(j):
        return {"fsdp": xor(chip, j) * 2 + core, "space": space}

    def row_mate(j):
        return {"fsdp": fsdp, "space": xor(row, j) * 4 + col}

    def col_mate(j):
        return {"fsdp": fsdp, "space": row * 4 + xor(col, j)}

    below = {"fsdp": fsdp, "space": lax.rem(space + 31, 32)}
    above = {"fsdp": fsdp, "space": lax.rem(space + 1, 32)}

    mates = (
        [sibling, below, above]
        + [chip_mate(j) for j in range(1, 8)]
        + [row_mate(j) for j in range(1, 8)]
        + [col_mate(j) for j in range(1, 4)]
    )
    barrier = pltpu.get_barrier_semaphore()
    for mate in mates:
        pl.semaphore_signal(barrier, inc=1, device_id=mate, device_id_type=MESH)

    sent = []

    saves = [
        pltpu.make_async_copy(src, dst, save_sem.at[i])
        for i, (src, dst) in enumerate((
            (bout_ref, bout_hbm), (gin_ref, gin_hbm), (gone_ref, gone_hbm), (gtwo_ref, gtwo_hbm),
        ))
    ]

    def send(src, dst, send_sem, recv_sem, device):
        copy = pltpu.make_async_remote_copy(
            src_ref=src, dst_ref=dst, send_sem=send_sem, recv_sem=recv_sem,
            device_id=device, device_id_type=MESH,
        )
        copy.start()
        sent.append(copy)
        return copy

    for k, ref in enumerate((wone_ref, wtwo_ref)):
        loads[k].wait()
        rows = ref[...].astype(F32)
        gap = jnp.zeros((6, KP - KA), F32)
        parts = []
        for a in range(3):
            parts += [rows[:, a * KA : (a + 1) * KA], gap]
        flat = jnp.concatenate(parts + [jnp.zeros((6, LT), F32)], axis=1)
        flat = jnp.concatenate([flat, jnp.zeros((2, 2 * HALF), F32)], axis=0)
        w_buf[k, 0] = jnp.concatenate([flat[:, :HALF], flat[:, HALF:]], axis=0).astype(BF16)

    pl.semaphore_wait(barrier, len(mates))

    w_copy, f_copy = [], []
    for k in range(2):
        own = [send(w_buf.at[k, 0], w_buf.at[k, 8], f_send.at[k, 0], f_recv.at[k, 0], sibling)]
        f_copy.append(own)
        w_copy.append({
            j: send(w_buf.at[k, 0], w_buf.at[k, j], w_send.at[k, j - 1], w_recv.at[k, j - 1], chip_mate(j))
            for j in FAR_FIRST
        })

    def forward_weight(k):
        for j in reversed(FAR_FIRST):
            w_copy[k][j].wait_recv()
            f_copy[k].append(
                send(w_buf.at[k, j], w_buf.at[k, 8 + j], f_send.at[k, j], f_recv.at[k, j], sibling)
            )

    for copy in loads[2:]:
        copy.wait()

    lane = lax.broadcasted_iota(jnp.int32, (1, LT), 1)
    z_pos, y_pos = lane & 7, (lane >> 3) & 7
    low = lane < 64

    def flag(cond):
        return jnp.where(cond, 1.0, 0.0).astype(F32)

    def named(face):
        return jnp.where(near_ref[0, 0, face] >= 0, 1.0, 0.0).astype(F32)

    occupied = jnp.where(live_ref[0, 0] > 0, 1.0, 0.0).astype(F32)
    low_f, high_f = flag(low), flag(lane >= 64)
    in_z = {c: flag((z_pos + c - 1 >= 0) & (z_pos + c - 1 < 8)) for c in (0, 2)}
    in_y = {b: flag((y_pos + b - 1 >= 0) & (y_pos + b - 1 < 8)) for b in (0, 2)}

    def wide(mask):
        return jnp.broadcast_to(mask, (CH, LT)).astype(BF16)

    inside = {"low": high_f, "mid": jnp.ones((1, LT), F32), "high": low_f}
    z_keep = {c: wide(in_z[c]) for c in (0, 2)}
    y_keep = {b: wide(in_y[b]) for b in (0, 2)}
    z_wrap = {
        (c, w): wide((1.0 - in_z[c]) * named(4 + c // 2) * inside[w]) for c in (0, 2) for w in inside
    }
    y_wrap = {}
    for b in (0, 2):
        for w in inside:
            base = (1.0 - in_y[b]) * named(2 + b // 2) * inside[w]
            for c in range(3):
                y_wrap[b, c, w] = wide(base if c == 1 else base * in_z[c])

    def unroll_tile(which, j, tile):
        w = "low" if j == 0 else "high" if j == 5 else "mid"
        for c in range(3):
            if c == 1:
                along = tile
            else:
                dz = c - 1
                along = (
                    pltpu.roll(tile, -dz % LT, 1) * z_keep[c]
                    + pltpu.roll(tile, 7 * dz % LT, 1) * z_wrap[c, w]
                )
            for b in range(3):
                if b == 1:
                    both = along
                else:
                    dy = b - 1
                    both = (
                        pltpu.roll(along, -8 * dy % LT, 1) * y_keep[b]
                        + pltpu.roll(along, 56 * dy % LT, 1) * y_wrap[b, c, w]
                    )
                tap = b * 3 + c
                cols[which, tap * CH : (tap + 1) * CH, j * LT : (j + 1) * LT] = both

    halo_copy = {}

    def send_halo(which, first, last):
        halo_out[which, 0] = half_turn(first)
        halo_out[which, 1] = half_turn(last)
        halo_copy[which] = [
            send(halo_out.at[which, 0], halo_in.at[which, 0], halo_send.at[which, 0],
                 halo_recv.at[which, 0], below),
            send(halo_out.at[which, 1], halo_in.at[which, 1], halo_send.at[which, 1],
                 halo_recv.at[which, 1], above),
        ]

    def unroll_middle(which, tiles):
        cols[which, KA:KP, :] = jnp.zeros((KP - KA, 6 * LT), BF16)
        for j in range(4):
            unroll_tile(which, j + 1, tiles[j])

    def unroll_edges(which):
        for copy in halo_copy[which]:
            copy.wait_recv()
        lower = halo_out[which, 1] * wide(high_f) + halo_in[which, 1] * wide(low_f * named(0))
        unroll_tile(which, 0, lower)
        upper = halo_out[which, 0] * wide(low_f) + halo_in[which, 0] * wide(high_f * named(1))
        unroll_tile(which, 5, upper)

    def lanes_of(array, j):
        return array[:, j * LT : (j + 1) * LT]

    x_tiles = paired([feat_ref[0, 0, :, j * LT : (j + 1) * LT].astype(F32) for j in range(4)], low)
    a_one = []
    for j in range(4):
        norm, scale = normalized(x_tiles[j])
        x_buf[0, j] = x_tiles[j]
        n_buf[0, j], r_buf[0, j] = norm, scale
        a_one.append((occupied * (norm * sigmoid(norm))).astype(BF16))
    send_halo(0, a_one[0], a_one[3])
    g_tiles = paired([grad_ref[0, 0, :, j * LT : (j + 1) * LT].astype(F32) for j in range(4)], low)
    g_two = []
    for j in range(4):
        x_buf[1, j] = g_tiles[j]
        g_two.append((occupied * g_tiles[j]).astype(BF16))
    send_halo(1, g_two[0], g_two[3])
    unroll_middle(0, a_one)
    unroll_middle(1, g_two)

    r_row = lax.broadcasted_iota(jnp.int32, (LT, CH), 0)
    r_col = lax.broadcasted_iota(jnp.int32, (LT, CH), 1)
    r_core = core + (r_row >> 6) * (1 - 2 * core)
    r_owner = (((r_row >> 3) & 7) ^ chip) * 2 + r_core
    spread = jnp.where(((r_row & 7) < 6) & (r_owner * 6 + (r_row & 7) == r_col), 1.0, 0.0).astype(BF16)

    def spread_rows(tiles):
        whole_g = jnp.concatenate(list(tiles), axis=1)
        return jnp.dot(spread, whole_g, preferred_element_type=F32).astype(BF16)

    gp_buf[1] = spread_rows(g_two)

    p_row = lax.broadcasted_iota(jnp.int32, (2 * CH, 256), 0)
    p_col = lax.broadcasted_iota(jnp.int32, (2 * CH, 256), 1)
    p_half = jnp.where(p_row >= CH, 1, 0)
    p_out = p_row - CH * p_half
    p_owner = (p_out * 43691) >> 18
    p_slot = ((p_owner >> 1) ^ chip) + 8 * ((p_owner & 1) ^ core)
    pick = jnp.where(p_slot * 16 + p_half * 8 + (p_out - 6 * p_owner) == p_col, 1.0, 0.0).astype(BF16)

    def assemble(k):
        for copy in f_copy[k]:
            copy.wait_recv()
        packed = w_buf[k].reshape(256, HALF)
        both = jnp.dot(pick, packed, preferred_element_type=F32).astype(BF16)
        w_full[k, :, :HALF] = both[:CH]
        w_full[k, :, HALF:] = both[CH:]

    def flip(k):
        for a in range(3):
            turned = jnp.transpose(w_full[k, :, (2 - a) * KP : (3 - a) * KP])
            blocks = [turned[(8 - t) * CH : (9 - t) * CH, :] for t in range(9)]
            w_flip[k, :, a * KP : (a + 1) * KP] = jnp.concatenate(
                blocks + [jnp.zeros((CH, KP - KA), BF16)], axis=1
            )

    def convolve(weights, k, which):
        total = None
        for a in range(3):
            part = jnp.dot(
                weights[k, :, a * KP : (a + 1) * KP],
                cols[which, :, a * LT : a * LT + 512],
                preferred_element_type=F32,
            )
            total = part if total is None else total + part
        return total

    one_copy, two_copy, y_copy, z_copy, g_copy = {}, {}, {}, {}, {}

    def start_term(m, which):
        term[m, :, 3 * KP :] = jnp.zeros((64, LT), F32)
        one_copy[m] = []
        for a in range(3):
            part = lax.dot_general(
                gp_buf[m], cols[which, :, a * LT : a * LT + 512],
                (((1,), (1,)), ((), ())), preferred_element_type=F32,
            )
            one_out[m, a] = part[64:].astype(BF16)
            one_copy[m].append(
                send(one_out.at[m, a], one_in.at[m, a], one_send.at[m, a], one_recv.at[m, a], sibling)
            )
            term[m, :, a * KP : (a + 1) * KP] = part[:64]

    def reduce_chips(m):
        for a in range(3):
            one_copy[m][a].wait_recv()
            term[m, :, a * KP : (a + 1) * KP] += one_in[m, a].astype(F32)
        two_copy[m] = {}
        for j in FAR_FIRST:
            two_out[m, j - 1] = jnp.concatenate(
                [term[m, 8 * j : 8 * j + 8, :HALF], term[m, 8 * j : 8 * j + 8, HALF:]], axis=0
            ).astype(BF16)
            two_copy[m][j] = send(
                two_out.at[m, j - 1], two_in.at[m, j - 1], two_send.at[m, j - 1],
                two_recv.at[m, j - 1], chip_mate(j),
            )

    def reduce_rows(m):
        total = jnp.concatenate([term[m, :8, :HALF], term[m, :8, HALF:]], axis=0)
        for j in reversed(FAR_FIRST):
            two_copy[m][j].wait_recv()
            total = total + two_in[m, j - 1].astype(F32)
        tiles = [total[:8, n * LT : (n + 1) * LT] for n in range(11)]
        tiles += [total[8:, n * LT : (n + 1) * LT] for n in range(10)]
        for p in range(7):
            sum_src[m, p] = jnp.concatenate(tiles[3 * p : 3 * p + 3], axis=1)
        sum_src[m, 7] = jnp.zeros((8, 3 * LT), F32)
        y_copy[m] = [
            send(sum_src.at[m, xor(row, j)], sum_in.at[m, j - 1], y_send.at[m, j - 1],
                 y_recv.at[m, j - 1], row_mate(j))
            for j in range(1, 8)
        ]

    def reduce_cols(m):
        total = sum_src[m, row]
        for j in range(1, 8):
            y_copy[m][j - 1].wait_recv()
            total = total + sum_in[m, j - 1]
        piece[m] = total
        z_copy[m] = [
            send(piece.at[m], piece_in.at[m, j - 1], z_send.at[m, j - 1], z_recv.at[m, j - 1], col_mate(j))
            for j in range(1, 4)
        ]

    def share_rows(m):
        for copy in z_copy[m]:
            copy.wait_recv()
        whole[m, row] = (piece[m] + piece_in[m, 0]) + (piece_in[m, 1] + piece_in[m, 2])
        g_copy[m] = [
            send(whole.at[m, row], whole.at[m, row], g_send.at[m, j - 1], g_recv.at[m, j - 1], row_mate(j))
            for j in range(1, 8)
        ]

    def finish(m, out_ref):
        for copy in g_copy[m]:
            copy.wait_recv()
        flat = jnp.concatenate([whole[m, p][:6] for p in range(7)], axis=1)
        out_ref[...] = jnp.concatenate([flat[:, a * KP : a * KP + KA] for a in range(3)], axis=1)

    def silu_tiles(hidden):
        tiles = []
        for j in range(4):
            norm, scale = normalized(lanes_of(hidden, j))
            n_buf[1, j], r_buf[1, j] = norm, scale
            tiles.append((occupied * (norm * sigmoid(norm))).astype(BF16))
        return tiles

    unroll_edges(0)
    unroll_edges(1)
    forward_weight(0)
    assemble(0)
    a_two = silu_tiles(convolve(w_full, 0, 0))
    send_halo(2, a_two[0], a_two[3])
    forward_weight(1)
    unroll_middle(2, a_two)
    assemble(1)
    flip(1)
    back = convolve(w_flip, 1, 1)
    g_one = []
    for j in range(4):
        inner = act_vjp(n_buf[1, j], r_buf[1, j], occupied * lanes_of(back, j))
        g_one.append((occupied * inner).astype(BF16))
    send_halo(3, g_one[0], g_one[3])
    gp_buf[0] = spread_rows(g_one)
    start_term(0, 0)
    unroll_edges(2)
    start_term(1, 2)
    reduce_chips(0)
    reduce_chips(1)

    unroll_middle(3, g_one)
    branch = convolve(w_full, 1, 2)
    outs = unpaired([occupied * (x_buf[0, j] + lanes_of(branch, j)) for j in range(4)], low)
    for j in range(4):
        bout_ref[0, 0, :, j * LT : (j + 1) * LT] = outs[j].astype(BF16)
    saves[0].start()
    flip(0)
    reduce_rows(0)
    reduce_rows(1)
    unroll_edges(3)
    back = convolve(w_flip, 0, 3)
    reduce_cols(0)
    reduce_cols(1)
    outs = []
    for j in range(4):
        inner = act_vjp(n_buf[0, j], r_buf[0, j], occupied * lanes_of(back, j))
        outs.append(occupied * (x_buf[1, j] + inner))
    outs = unpaired(outs, low)
    for j in range(4):
        gin_ref[0, 0, :, j * LT : (j + 1) * LT] = outs[j].astype(BF16)
    saves[1].start()
    share_rows(0)
    share_rows(1)
    finish(0, gone_ref)
    saves[2].start()
    finish(1, gtwo_ref)
    saves[3].start()
    for copy in sent:
        copy.wait_send()
    for copy in saves:
        copy.wait()


def store(*refs):
    copies = [pltpu.make_async_copy(refs[i], refs[4 + i], refs[8].at[i]) for i in range(4)]
    for copy in copies:
        copy.start()
    for copy in copies:
        copy.wait()


def body(features, w_first, w_second, neighbours, live_counts, output_gradient):
    dma = pltpu.SemaphoreType.DMA
    vmem = pl.BlockSpec(memory_space=pltpu.VMEM)
    hbm = pl.BlockSpec(memory_space=pltpu.HBM)
    results = pl.pallas_call(
        kernel,
        out_shape=(
            jax.ShapeDtypeStruct(features.shape, BF16),
            jax.ShapeDtypeStruct(features.shape, BF16),
            jax.ShapeDtypeStruct(w_first.shape, F32),
            jax.ShapeDtypeStruct(w_second.shape, F32),
        ),
        in_specs=[hbm] * 6,
        out_specs=(hbm,) * 4,
        scratch_shapes=[
            pltpu.VMEM(features.shape, BF16),
            pltpu.VMEM(features.shape, BF16),
            pltpu.VMEM(w_first.shape, F32),
            pltpu.VMEM(w_second.shape, F32),
            pltpu.VMEM(features.shape, BF16),
            pltpu.VMEM(w_first.shape, BF16),
            pltpu.VMEM(w_second.shape, BF16),
            pltpu.SMEM(neighbours.shape, jnp.int32),
            pltpu.SMEM(live_counts.shape, jnp.int32),
            pltpu.VMEM(features.shape, BF16),
            dma((6,)),
            dma((4,)),
            pltpu.VMEM((2, 16, 16, HALF), BF16),
            pltpu.VMEM((2, CH, 2 * HALF), BF16),
            pltpu.VMEM((2, CH, 3 * KP), BF16),
            pltpu.VMEM((4, 2, CH, LT), BF16),
            pltpu.VMEM((4, 2, CH, LT), BF16),
            pltpu.VMEM((4, KP, 6 * LT), BF16),
            pltpu.VMEM((2, 4, CH, LT), F32),
            pltpu.VMEM((2, 4, CH, LT), F32),
            pltpu.VMEM((2, 4, 1, LT), F32),
            pltpu.VMEM((2, LT, 512), BF16),
            pltpu.VMEM((2, 64, 2 * HALF), F32),
            pltpu.VMEM((2, 3, 64, KP), BF16),
            pltpu.VMEM((2, 3, 64, KP), BF16),
            pltpu.VMEM((2, 7, 16, HALF), BF16),
            pltpu.VMEM((2, 7, 16, HALF), BF16),
            pltpu.VMEM((2, 8, 8, 3 * LT), F32),
            pltpu.VMEM((2, 7, 8, 3 * LT), F32),
            pltpu.VMEM((2, 8, 3 * LT), F32),
            pltpu.VMEM((2, 3, 8, 3 * LT), F32),
            pltpu.VMEM((2, 8, 8, 3 * LT), F32),
            dma((2, 7)), dma((2, 7)), dma((2, 8)), dma((2, 8)), dma((4, 2)), dma((4, 2)),
            dma((2, 3)), dma((2, 3)), dma((2, 7)), dma((2, 7)), dma((2, 7)), dma((2, 7)),
            dma((2, 3)), dma((2, 3)), dma((2, 7)), dma((2, 7)),
        ],
        compiler_params=pltpu.CompilerParams(
            collective_id=0, has_side_effects=True, vmem_limit_bytes=63 * 1024 * 1024
        ),
    )(features, w_first, w_second, neighbours, live_counts, output_gradient)
    return pl.pallas_call(
        store,
        out_shape=tuple(jax.ShapeDtypeStruct(r.shape, r.dtype) for r in results),
        in_specs=[vmem] * 4,
        out_specs=(hbm,) * 4,
        scratch_shapes=[dma((4,))],
        compiler_params=pltpu.CompilerParams(vmem_limit_bytes=63 * 1024 * 1024),
    )(*results)


def solution(mesh):
    blocks = P("fsdp", "space", None, None)
    weights = P("fsdp", None)
    return jax.shard_map(
        body,
        mesh=mesh,
        in_specs=(blocks, weights, weights, P("fsdp", "space", None), P("fsdp", "space"), blocks),
        out_specs=(blocks, blocks, weights, weights),
        check_vma=False,
    )
```

```python
import jax
import jax.numpy as jnp
from jax import lax
from jax.experimental import pallas as pl
from jax.experimental.pallas import tpu as pltpu
from jax.sharding import PartitionSpec as P

MESH = pl.DeviceIdType.MESH
F32 = jnp.float32
BF16 = jnp.bfloat16

CH = 96
LT = 128
KA = 9 * CH
KP = 896
HALF = 11 * LT
EPS = 1e-05
WHOLE = BF16
FAR_FIRST = (6, 2, 7, 5, 3, 1, 4)


def xor(value, pattern):
    for bit in (1, 2, 4):
        if pattern & bit:
            value = value + (1 - 2 * lax.rem(lax.div(value, bit), 2)) * bit
    return value


def half_turn(tile):
    return pltpu.roll(tile, 64, 1)


def paired(tiles, low):
    t0, t1, t2, t3 = tiles
    return (
        jnp.where(low, t0, half_turn(t2)),
        jnp.where(low, half_turn(t0), t2),
        jnp.where(low, t1, half_turn(t3)),
        jnp.where(low, half_turn(t1), t3),
    )


def unpaired(tiles, low):
    p0, p1, p2, p3 = tiles
    return (
        jnp.where(low, p0, half_turn(p1)),
        jnp.where(low, p2, half_turn(p3)),
        jnp.where(low, half_turn(p0), p1),
        jnp.where(low, half_turn(p2), p3),
    )


def normalized(u):
    centred = u - jnp.mean(u, axis=0, keepdims=True)
    scale = lax.rsqrt(jnp.mean(centred * centred, axis=0, keepdims=True) + EPS)
    return centred * scale, scale


def sigmoid(v):
    return 1.0 / (1.0 + jnp.exp(-v))


def act_vjp(norm, scale, cotangent):
    gate = sigmoid(norm)
    inner = cotangent * (gate * (1.0 + norm * (1.0 - gate)))
    return scale * (
        inner
        - jnp.mean(inner, axis=0, keepdims=True)
        - norm * jnp.mean(inner * norm, axis=0, keepdims=True)
    )


def kernel(
    feat_hbm, wone_hbm, wtwo_hbm, near_hbm, live_hbm, grad_hbm,
    bout_hbm, gin_hbm, gone_hbm, gtwo_hbm,
    bout_ref, gin_ref, gone_ref, gtwo_ref, feat_ref, wone_ref, wtwo_ref, near_ref, live_ref, grad_ref, load_sem, save_sem,
    w_buf, w_full, w_flip, halo_out, halo_in, cols, x_buf, n_buf, r_buf, gp_buf, gp_wide,
    term, one_out, one_in, two_out, two_in, own_sum, sum_src, sum_in, piece, piece_in, whole,
    w_send, w_recv, f_send, f_recv, halo_send, halo_recv,
    one_send, one_recv, two_send, two_recv, y_send, y_recv, z_send, z_recv, g_send, g_recv,
):
    loads = [
        pltpu.make_async_copy(src, dst, load_sem.at[i])
        for i, (src, dst) in enumerate((
            (wone_hbm, wone_ref), (wtwo_hbm, wtwo_ref), (feat_hbm, feat_ref),
            (near_hbm, near_ref), (live_hbm, live_ref), (grad_hbm, grad_ref),
        ))
    ]
    for copy in loads:
        copy.start()
    fsdp = lax.axis_index("fsdp")
    space = lax.axis_index("space")
    chip, core = lax.div(fsdp, 2), lax.rem(fsdp, 2)
    row, col = lax.div(space, 4), lax.rem(space, 4)
    sibling = {"fsdp": chip * 2 + (1 - core), "space": space}

    def chip_mate(j):
        return {"fsdp": xor(chip, j) * 2 + core, "space": space}

    def row_mate(j):
        return {"fsdp": fsdp, "space": xor(row, j) * 4 + col}

    def col_mate(j):
        return {"fsdp": fsdp, "space": row * 4 + xor(col, j)}

    below = {"fsdp": fsdp, "space": lax.rem(space + 31, 32)}
    above = {"fsdp": fsdp, "space": lax.rem(space + 1, 32)}

    mates = (
        [sibling, below, above]
        + [chip_mate(j) for j in range(1, 8)]
        + [row_mate(j) for j in range(1, 8)]
        + [col_mate(j) for j in range(1, 4)]
    )
    barrier = pltpu.get_barrier_semaphore()
    for mate in mates:
        pl.semaphore_signal(barrier, inc=1, device_id=mate, device_id_type=MESH)

    sent = []

    saves = [
        pltpu.make_async_copy(src, dst, save_sem.at[i])
        for i, (src, dst) in enumerate((
            (bout_ref, bout_hbm), (gin_ref, gin_hbm), (gone_ref, gone_hbm), (gtwo_ref, gtwo_hbm),
        ))
    ]

    def send(src, dst, send_sem, recv_sem, device):
        copy = pltpu.make_async_remote_copy(
            src_ref=src, dst_ref=dst, send_sem=send_sem, recv_sem=recv_sem,
            device_id=device, device_id_type=MESH,
        )
        copy.start()
        sent.append(copy)
        return copy

    for k, ref in enumerate((wone_ref, wtwo_ref)):
        loads[k].wait()
        rows = ref[...].astype(F32)
        gap = jnp.zeros((6, KP - KA), F32)
        parts = []
        for a in range(3):
            parts += [rows[:, a * KA : (a + 1) * KA], gap]
        flat = jnp.concatenate(parts + [jnp.zeros((6, LT), F32)], axis=1)
        flat = jnp.concatenate([flat, jnp.zeros((2, 2 * HALF), F32)], axis=0)
        w_buf[k, 0] = jnp.concatenate([flat[:, :HALF], flat[:, HALF:]], axis=0).astype(BF16)

    pl.semaphore_wait(barrier, len(mates))

    w_copy, f_copy = [], []
    for k in range(2):
        own = [send(w_buf.at[k, 0], w_buf.at[k, 8], f_send.at[k, 0], f_recv.at[k, 0], sibling)]
        f_copy.append(own)
        w_copy.append({
            j: send(w_buf.at[k, 0], w_buf.at[k, j], w_send.at[k, j - 1], w_recv.at[k, j - 1], chip_mate(j))
            for j in FAR_FIRST
        })

    def forward_weight(k):
        for j in reversed(FAR_FIRST):
            w_copy[k][j].wait_recv()
            f_copy[k].append(
                send(w_buf.at[k, j], w_buf.at[k, 8 + j], f_send.at[k, j], f_recv.at[k, j], sibling)
            )

    for copy in loads[2:]:
        copy.wait()

    lane = lax.broadcasted_iota(jnp.int32, (1, LT), 1)
    z_pos, y_pos = lane & 7, (lane >> 3) & 7
    low = lane < 64

    def flag(cond):
        return jnp.where(cond, 1.0, 0.0).astype(F32)

    def named(face):
        return jnp.where(near_ref[0, 0, face] >= 0, 1.0, 0.0).astype(F32)

    occupied = jnp.where(live_ref[0, 0] > 0, 1.0, 0.0).astype(F32)
    low_f, high_f = flag(low), flag(lane >= 64)
    in_z = {c: flag((z_pos + c - 1 >= 0) & (z_pos + c - 1 < 8)) for c in (0, 2)}
    in_y = {b: flag((y_pos + b - 1 >= 0) & (y_pos + b - 1 < 8)) for b in (0, 2)}

    def wide(mask):
        return jnp.broadcast_to(mask, (CH, LT)).astype(BF16)

    inside = {"low": high_f, "mid": jnp.ones((1, LT), F32), "high": low_f, "edge": jnp.zeros((1, LT), F32)}
    z_keep = {c: wide(in_z[c]) for c in (0, 2)}
    y_keep = {b: wide(in_y[b]) for b in (0, 2)}
    z_wrap = {
        (c, w): wide((1.0 - in_z[c]) * named(4 + c // 2) * inside[w]) for c in (0, 2) for w in inside
    }
    y_wrap = {}
    for b in (0, 2):
        for w in inside:
            base = (1.0 - in_y[b]) * named(2 + b // 2) * inside[w]
            for c in range(3):
                y_wrap[b, c, w] = wide(base if c == 1 else base * in_z[c])

    def unroll_tile(which, j, tile, w=None):
        w = w or ("low" if j == 0 else "high" if j == 5 else "mid")
        for c in range(3):
            if c == 1:
                along = tile
            else:
                dz = c - 1
                along = (
                    pltpu.roll(tile, -dz % LT, 1) * z_keep[c]
                    + pltpu.roll(tile, 7 * dz % LT, 1) * z_wrap[c, w]
                )
            for b in range(3):
                if b == 1:
                    both = along
                else:
                    dy = b - 1
                    both = (
                        pltpu.roll(along, -8 * dy % LT, 1) * y_keep[b]
                        + pltpu.roll(along, 56 * dy % LT, 1) * y_wrap[b, c, w]
                    )
                tap = b * 3 + c
                cols[which, tap * CH : (tap + 1) * CH, j * LT : (j + 1) * LT] = both

    halo_copy = {}

    def send_halo(which, first, last):
        halo_out[which, 0] = half_turn(first)
        halo_out[which, 1] = half_turn(last)
        halo_copy[which] = [
            send(halo_out.at[which, 0], halo_in.at[which, 0], halo_send.at[which, 0],
                 halo_recv.at[which, 0], below),
            send(halo_out.at[which, 1], halo_in.at[which, 1], halo_send.at[which, 1],
                 halo_recv.at[which, 1], above),
        ]

    def unroll_middle(which, tiles):
        cols[which, KA:KP, :] = jnp.zeros((KP - KA, 6 * LT), BF16)
        for j in range(4):
            unroll_tile(which, j + 1, tiles[j])

    def unroll_edges(which):
        for copy in halo_copy[which]:
            copy.wait_recv()
        lower = halo_out[which, 1] * wide(high_f) + halo_in[which, 1] * wide(low_f * named(0))
        unroll_tile(which, 0, lower)
        upper = halo_out[which, 0] * wide(low_f) + halo_in[which, 0] * wide(high_f * named(1))
        unroll_tile(which, 5, upper)

    def lanes_of(array, j):
        return array[:, j * LT : (j + 1) * LT]

    x_tiles = paired([feat_ref[0, 0, :, j * LT : (j + 1) * LT].astype(F32) for j in range(4)], low)
    a_one = []
    for j in range(4):
        norm, scale = normalized(x_tiles[j])
        x_buf[0, j] = x_tiles[j]
        n_buf[0, j], r_buf[0, j] = norm, scale
        a_one.append((occupied * (norm * sigmoid(norm))).astype(BF16))
    send_halo(0, a_one[0], a_one[3])
    g_tiles = paired([grad_ref[0, 0, :, j * LT : (j + 1) * LT].astype(F32) for j in range(4)], low)
    g_two = []
    for j in range(4):
        x_buf[1, j] = g_tiles[j]
        g_two.append((occupied * g_tiles[j]).astype(BF16))
    send_halo(1, g_two[0], g_two[3])
    unroll_middle(0, a_one)
    unroll_middle(1, g_two)

    r_row = lax.broadcasted_iota(jnp.int32, (LT, CH), 0)
    r_col = lax.broadcasted_iota(jnp.int32, (LT, CH), 1)
    r_core = core + (r_row >> 6) * (1 - 2 * core)
    r_owner = (((r_row >> 3) & 7) ^ chip) * 2 + r_core
    spread = jnp.where(((r_row & 7) < 6) & (r_owner * 6 + (r_row & 7) == r_col), 1.0, 0.0).astype(BF16)

    def spread_rows(tiles):
        whole_g = jnp.concatenate(list(tiles), axis=1)
        return jnp.dot(spread, whole_g, preferred_element_type=F32).astype(BF16)

    p_row = lax.broadcasted_iota(jnp.int32, (2 * CH, 256), 0)
    p_col = lax.broadcasted_iota(jnp.int32, (2 * CH, 256), 1)
    p_half = jnp.where(p_row >= CH, 1, 0)
    p_out = p_row - CH * p_half
    p_owner = (p_out * 43691) >> 18
    p_slot = ((p_owner >> 1) ^ chip) + 8 * ((p_owner & 1) ^ core)
    pick = jnp.where(p_slot * 16 + p_half * 8 + (p_out - 6 * p_owner) == p_col, 1.0, 0.0).astype(BF16)

    def assemble(k):
        for copy in f_copy[k]:
            copy.wait_recv()
        packed = w_buf[k].reshape(256, HALF)
        both = jnp.dot(pick, packed, preferred_element_type=F32).astype(BF16)
        w_full[k, :, :HALF] = both[:CH]
        w_full[k, :, HALF:] = both[CH:]

    def flip(k):
        for a in range(3):
            turned = jnp.transpose(w_full[k, :, (2 - a) * KP : (3 - a) * KP])
            blocks = [turned[(8 - t) * CH : (9 - t) * CH, :] for t in range(9)]
            w_flip[k, :, a * KP : (a + 1) * KP] = jnp.concatenate(
                blocks + [jnp.zeros((CH, KP - KA), BF16)], axis=1
            )

    def convolve(weights, k, which):
        total = None
        for a in range(3):
            part = jnp.dot(
                weights[k, :, a * KP : (a + 1) * KP],
                cols[which, :, a * LT : a * LT + 512],
                preferred_element_type=F32,
            )
            total = part if total is None else total + part
        return total

    one_copy, two_copy = {}, {}

    def first_pair(a):
        return gp_buf[...], cols[0, :, a * LT : a * LT + 512]

    def second_pair(a):
        if a == 0:
            return gp_wide[:, 2 * LT : 7 * LT], cols[2, :, LT : 6 * LT]
        if a == 1:
            return gp_wide[:, LT : 5 * LT], cols[2, :, LT : 5 * LT]
        left = jnp.concatenate([gp_wide[:, : 4 * LT], gp_wide[:, 7 * LT :]], axis=1)
        return left, cols[2, :, LT : 6 * LT]

    def start_term(m, pair):
        term[m, :, 3 * KP :] = jnp.zeros((64, LT), F32)
        one_copy[m] = []
        for a in range(3):
            part = lax.dot_general(
                *pair(a),
                (((1,), (1,)), ((), ())), preferred_element_type=F32,
            )
            one_out[m, a] = part[64:].astype(BF16)
            one_copy[m].append(
                send(one_out.at[m, a], one_in.at[m, a], one_send.at[m, a], one_recv.at[m, a], sibling)
            )
            term[m, :, a * KP : (a + 1) * KP] = part[:64]

    def reduce_chips(m):
        for a in range(3):
            one_copy[m][a].wait_recv()
            term[m, :, a * KP : (a + 1) * KP] += one_in[m, a].astype(F32)
        two_copy[m] = {}
        for j in FAR_FIRST:
            two_out[m, j - 1] = jnp.concatenate(
                [term[m, 8 * j : 8 * j + 8, :HALF], term[m, 8 * j : 8 * j + 8, HALF:]], axis=0
            ).astype(BF16)
            two_copy[m][j] = send(
                two_out.at[m, j - 1], two_in.at[m, j - 1], two_send.at[m, j - 1],
                two_recv.at[m, j - 1], chip_mate(j),
            )

    def sum_chips(m):
        total = jnp.concatenate([term[m, :8, :HALF], term[m, :8, HALF:]], axis=0)
        for j in reversed(FAR_FIRST):
            two_copy[m][j].wait_recv()
            total = total + two_in[m, j - 1].astype(F32)
        tiles = [total[:8, n * LT : (n + 1) * LT] for n in range(11)]
        return tiles + [total[8:, n * LT : (n + 1) * LT] for n in range(10)]

    rows_far_first = (4, 5, 3, 2, 6, 7, 1)
    later = {}

    def reduce_rows():
        other = sum_chips(1)
        both = [sum_chips(0), other]
        for p in range(7):
            joined = jnp.concatenate(
                [jnp.concatenate(tiles[3 * p : 3 * p + 3], axis=1) for tiles in both], axis=0
            )
            own_sum[p] = joined
            sum_src[p] = joined.astype(BF16)
        own_sum[7] = jnp.zeros((16, 3 * LT), F32)
        sum_src[7] = jnp.zeros((16, 3 * LT), BF16)
        later["y"] = [
            send(sum_src.at[xor(row, j)], sum_in.at[j - 1], y_send.at[j - 1], y_recv.at[j - 1], row_mate(j))
            for j in rows_far_first
        ]

    def reduce_cols():
        for copy in later["y"]:
            copy.wait_recv()
        total = own_sum[row]
        for j in range(7):
            total = total + sum_in[j].astype(F32)
        piece[...] = total.astype(BF16)
        later["z"] = [
            send(piece, piece_in.at[j - 1], z_send.at[j - 1], z_recv.at[j - 1], col_mate(j))
            for j in (2, 3, 1)
        ]

    def share_rows():
        for copy in later["z"]:
            copy.wait_recv()
        parts = [piece[...].astype(F32)] + [piece_in[j].astype(F32) for j in range(3)]
        whole[row] = ((parts[0] + parts[1]) + (parts[2] + parts[3])).astype(WHOLE)
        later["g"] = [
            send(whole.at[row], whole.at[row], g_send.at[j - 1], g_recv.at[j - 1], row_mate(j))
            for j in rows_far_first
        ]

    def finish():
        for copy in later["g"]:
            copy.wait_recv()
        pieces = [whole[p].astype(F32) for p in range(7)]
        for m, out_ref in enumerate((gone_ref, gtwo_ref)):
            flat = jnp.concatenate([one[8 * m : 8 * m + 6] for one in pieces], axis=1)
            out_ref[...] = jnp.concatenate([flat[:, a * KP : a * KP + KA] for a in range(3)], axis=1)

    def silu_tiles(hidden):
        tiles = []
        for j in range(4):
            norm, scale = normalized(lanes_of(hidden, j))
            n_buf[1, j], r_buf[1, j] = norm, scale
            tiles.append((occupied * (norm * sigmoid(norm))).astype(BF16))
        return tiles

    unroll_edges(0)
    unroll_edges(1)
    gp_wide[...] = spread_rows(
        [halo_out[1, 1] * wide(high_f)] + g_two + [halo_out[1, 0] * wide(low_f)]
        + [halo_in[1, 0] * wide(high_f * named(1)), halo_in[1, 1] * wide(low_f * named(0))]
    )
    forward_weight(0)
    forward_weight(1)
    assemble(0)
    a_two = silu_tiles(convolve(w_full, 0, 0))
    send_halo(2, a_two[0], a_two[3])
    unroll_middle(2, a_two)
    unroll_tile(2, 5, a_two[0] * wide(low_f) + a_two[3] * wide(high_f), "edge")
    start_term(1, second_pair)
    assemble(1)
    flip(1)
    back = convolve(w_flip, 1, 1)
    g_one = []
    for j in range(4):
        inner = act_vjp(n_buf[1, j], r_buf[1, j], occupied * lanes_of(back, j))
        g_one.append((occupied * inner).astype(BF16))
    send_halo(3, g_one[0], g_one[3])
    gp_buf[...] = spread_rows(g_one)
    start_term(0, first_pair)
    reduce_chips(1)
    reduce_chips(0)
    unroll_edges(2)

    unroll_middle(3, g_one)
    branch = convolve(w_full, 1, 2)
    outs = unpaired([occupied * (x_buf[0, j] + lanes_of(branch, j)) for j in range(4)], low)
    for j in range(4):
        bout_ref[0, 0, :, j * LT : (j + 1) * LT] = outs[j].astype(BF16)
    saves[0].start()
    flip(0)
    reduce_rows()
    unroll_edges(3)
    back = convolve(w_flip, 0, 3)
    reduce_cols()
    outs = []
    for j in range(4):
        inner = act_vjp(n_buf[0, j], r_buf[0, j], occupied * lanes_of(back, j))
        outs.append(occupied * (x_buf[1, j] + inner))
    outs = unpaired(outs, low)
    for j in range(4):
        gin_ref[0, 0, :, j * LT : (j + 1) * LT] = outs[j].astype(BF16)
    saves[1].start()
    share_rows()
    finish()
    saves[2].start()
    saves[3].start()
    for copy in sent:
        copy.wait_send()
    for copy in saves:
        copy.wait()


def store(*refs):
    copies = [pltpu.make_async_copy(refs[i], refs[4 + i], refs[8].at[i]) for i in range(4)]
    for copy in copies:
        copy.start()
    for copy in copies:
        copy.wait()


def body(features, w_first, w_second, neighbours, live_counts, output_gradient):
    dma = pltpu.SemaphoreType.DMA
    vmem = pl.BlockSpec(memory_space=pltpu.VMEM)
    hbm = pl.BlockSpec(memory_space=pltpu.HBM)
    results = pl.pallas_call(
        kernel,
        out_shape=(
            jax.ShapeDtypeStruct(features.shape, BF16),
            jax.ShapeDtypeStruct(features.shape, BF16),
            jax.ShapeDtypeStruct(w_first.shape, F32),
            jax.ShapeDtypeStruct(w_second.shape, F32),
        ),
        in_specs=[hbm] * 6,
        out_specs=(hbm,) * 4,
        scratch_shapes=[
            pltpu.VMEM(features.shape, BF16),
            pltpu.VMEM(features.shape, BF16),
            pltpu.VMEM(w_first.shape, F32),
            pltpu.VMEM(w_second.shape, F32),
            pltpu.VMEM(features.shape, BF16),
            pltpu.VMEM(w_first.shape, BF16),
            pltpu.VMEM(w_second.shape, BF16),
            pltpu.SMEM(neighbours.shape, jnp.int32),
            pltpu.SMEM(live_counts.shape, jnp.int32),
            pltpu.VMEM(features.shape, BF16),
            dma((6,)),
            dma((4,)),
            pltpu.VMEM((2, 16, 16, HALF), BF16),
            pltpu.VMEM((2, CH, 2 * HALF), BF16),
            pltpu.VMEM((2, CH, 3 * KP), BF16),
            pltpu.VMEM((4, 2, CH, LT), BF16),
            pltpu.VMEM((4, 2, CH, LT), BF16),
            pltpu.VMEM((4, KP, 6 * LT), BF16),
            pltpu.VMEM((2, 4, CH, LT), F32),
            pltpu.VMEM((2, 4, CH, LT), F32),
            pltpu.VMEM((2, 4, 1, LT), F32),
            pltpu.VMEM((LT, 512), BF16),
            pltpu.VMEM((LT, 8 * LT), BF16),
            pltpu.VMEM((2, 64, 2 * HALF), F32),
            pltpu.VMEM((2, 3, 64, KP), BF16),
            pltpu.VMEM((2, 3, 64, KP), BF16),
            pltpu.VMEM((2, 7, 16, HALF), BF16),
            pltpu.VMEM((2, 7, 16, HALF), BF16),
            pltpu.VMEM((8, 16, 3 * LT), F32),
            pltpu.VMEM((8, 16, 3 * LT), BF16),
            pltpu.VMEM((7, 16, 3 * LT), BF16),
            pltpu.VMEM((16, 3 * LT), BF16),
            pltpu.VMEM((3, 16, 3 * LT), BF16),
            pltpu.VMEM((8, 16, 3 * LT), WHOLE),
            dma((2, 7)), dma((2, 7)), dma((2, 8)), dma((2, 8)), dma((4, 2)), dma((4, 2)),
            dma((2, 3)), dma((2, 3)), dma((2, 7)), dma((2, 7)), dma((7,)), dma((7,)),
            dma((3,)), dma((3,)), dma((7,)), dma((7,)),
        ],
        compiler_params=pltpu.CompilerParams(
            collective_id=0, has_side_effects=True, vmem_limit_bytes=63 * 1024 * 1024
        ),
    )(features, w_first, w_second, neighbours, live_counts, output_gradient)
    return pl.pallas_call(
        store,
        out_shape=tuple(jax.ShapeDtypeStruct(r.shape, r.dtype) for r in results),
        in_specs=[vmem] * 4,
        out_specs=(hbm,) * 4,
        scratch_shapes=[dma((4,))],
        compiler_params=pltpu.CompilerParams(vmem_limit_bytes=63 * 1024 * 1024),
    )(*results)


def solution(mesh):
    blocks = P("fsdp", "space", None, None)
    weights = P("fsdp", None)
    return jax.shard_map(
        body,
        mesh=mesh,
        in_specs=(blocks, weights, weights, P("fsdp", "space", None), P("fsdp", "space"), blocks),
        out_specs=(blocks, blocks, weights, weights),
        check_vma=False,
    )
```

```python
import jax
import jax.numpy as jnp
from jax import lax
from jax.experimental import pallas as pl
from jax.experimental.pallas import tpu as pltpu
from jax.sharding import PartitionSpec as P

MESH = pl.DeviceIdType.MESH
F32 = jnp.float32
BF16 = jnp.bfloat16

CH = 96
LT = 128
KA = 9 * CH
KP = 896
EPS = 1e-05
WHOLE = BF16
FAR_FIRST = (6, 2, 7, 5, 3, 1, 4)


def xor(value, pattern):
    for bit in (1, 2, 4):
        if pattern & bit:
            value = value + (1 - 2 * lax.rem(lax.div(value, bit), 2)) * bit
    return value


def half_turn(tile):
    return pltpu.roll(tile, 64, 1)


def paired(tiles, low):
    t0, t1, t2, t3 = tiles
    return (
        jnp.where(low, t0, half_turn(t2)),
        jnp.where(low, half_turn(t0), t2),
        jnp.where(low, t1, half_turn(t3)),
        jnp.where(low, half_turn(t1), t3),
    )


def unpaired(tiles, low):
    p0, p1, p2, p3 = tiles
    return (
        jnp.where(low, p0, half_turn(p1)),
        jnp.where(low, p2, half_turn(p3)),
        jnp.where(low, half_turn(p0), p1),
        jnp.where(low, half_turn(p2), p3),
    )


def packed(rows):
    tail = [rows[:, n * LT : (n + 1) * LT] for n in range(16, 21)]
    blank = jnp.zeros((2, LT), rows.dtype)
    spare = jnp.concatenate(
        [
            jnp.concatenate([tail[0][4:6], tail[2][4:6], tail[4][4:6]], axis=1),
            jnp.concatenate([tail[1][4:6], tail[3][4:6], blank], axis=1),
        ],
        axis=0,
    )
    last = jnp.concatenate([rows[:4, 16 * LT :], spare], axis=1)
    return jnp.concatenate([rows[:, : 8 * LT], rows[:, 8 * LT : 16 * LT], last], axis=0)


def unpacked(block):
    tiles = [block[:6, n * LT : (n + 1) * LT] for n in range(8)]
    tiles += [block[6:12, n * LT : (n + 1) * LT] for n in range(8)]
    for n in range(5):
        top, col = 12 + 2 * (n % 2), 5 + n // 2
        tiles.append(
            jnp.concatenate(
                [block[12:16, n * LT : (n + 1) * LT], block[top : top + 2, col * LT : (col + 1) * LT]], axis=0
            )
        )
    return tiles


def normalized(u):
    centred = u - jnp.mean(u, axis=0, keepdims=True)
    scale = lax.rsqrt(jnp.mean(centred * centred, axis=0, keepdims=True) + EPS)
    return centred * scale, scale


def sigmoid(v):
    return 1.0 / (1.0 + jnp.exp(-v))


def act_vjp(norm, scale, cotangent):
    gate = sigmoid(norm)
    inner = cotangent * (gate * (1.0 + norm * (1.0 - gate)))
    return scale * (
        inner
        - jnp.mean(inner, axis=0, keepdims=True)
        - norm * jnp.mean(inner * norm, axis=0, keepdims=True)
    )


def kernel(
    feat_hbm, wone_hbm, wtwo_hbm, near_hbm, live_hbm, grad_hbm,
    bout_hbm, gin_hbm, gone_hbm, gtwo_hbm,
    bout_ref, gin_ref, gone_ref, gtwo_ref, feat_ref, wone_ref, wtwo_ref, near_ref, live_ref, grad_ref, load_sem, save_sem,
    w_buf, w_full, w_flip, halo_out, halo_in, cols, x_buf, n_buf, r_buf, gp_buf, gp_wide,
    term, one_out, one_in, two_out, two_in, own_sum, sum_src, sum_in, piece, piece_in, whole,
    w_send, w_recv, f_send, f_recv, halo_send, halo_recv,
    one_send, one_recv, two_send, two_recv, y_send, y_recv, z_send, z_recv, g_send, g_recv,
):
    loads = [
        pltpu.make_async_copy(src, dst, load_sem.at[i])
        for i, (src, dst) in enumerate((
            (wone_hbm, wone_ref), (wtwo_hbm, wtwo_ref), (feat_hbm, feat_ref),
            (near_hbm, near_ref), (live_hbm, live_ref), (grad_hbm, grad_ref),
        ))
    ]
    for copy in loads:
        copy.start()
    fsdp = lax.axis_index("fsdp")
    space = lax.axis_index("space")
    chip, core = lax.div(fsdp, 2), lax.rem(fsdp, 2)
    row, col = lax.div(space, 4), lax.rem(space, 4)
    sibling = {"fsdp": chip * 2 + (1 - core), "space": space}

    def chip_mate(j):
        return {"fsdp": xor(chip, j) * 2 + core, "space": space}

    def row_mate(j):
        return {"fsdp": fsdp, "space": xor(row, j) * 4 + col}

    def col_mate(j):
        return {"fsdp": fsdp, "space": row * 4 + xor(col, j)}

    below = {"fsdp": fsdp, "space": lax.rem(space + 31, 32)}
    above = {"fsdp": fsdp, "space": lax.rem(space + 1, 32)}

    mates = (
        [sibling, below, above]
        + [chip_mate(j) for j in range(1, 8)]
        + [row_mate(j) for j in range(1, 8)]
        + [col_mate(j) for j in range(1, 4)]
    )
    barrier = pltpu.get_barrier_semaphore()
    for mate in mates:
        pl.semaphore_signal(barrier, inc=1, device_id=mate, device_id_type=MESH)

    sent = []

    saves = [
        pltpu.make_async_copy(src, dst, save_sem.at[i])
        for i, (src, dst) in enumerate((
            (bout_ref, bout_hbm), (gin_ref, gin_hbm), (gone_ref, gone_hbm), (gtwo_ref, gtwo_hbm),
        ))
    ]

    def send(src, dst, send_sem, recv_sem, device):
        copy = pltpu.make_async_remote_copy(
            src_ref=src, dst_ref=dst, send_sem=send_sem, recv_sem=recv_sem,
            device_id=device, device_id_type=MESH,
        )
        copy.start()
        sent.append(copy)
        return copy

    for k, ref in enumerate((wone_ref, wtwo_ref)):
        loads[k].wait()
        rows = ref[...].astype(F32)
        gap = jnp.zeros((6, KP - KA), F32)
        parts = []
        for a in range(3):
            parts += [rows[:, a * KA : (a + 1) * KA], gap]
        w_buf[k, 0] = packed(jnp.concatenate(parts, axis=1)).astype(BF16)

    pl.semaphore_wait(barrier, len(mates))

    w_copy, f_copy = [], []
    for k in range(2):
        own = [send(w_buf.at[k, 0], w_buf.at[k, 8], f_send.at[k, 0], f_recv.at[k, 0], sibling)]
        f_copy.append(own)
        w_copy.append({
            j: send(w_buf.at[k, 0], w_buf.at[k, j], w_send.at[k, j - 1], w_recv.at[k, j - 1], chip_mate(j))
            for j in FAR_FIRST
        })

    def forward_weight(k):
        for j in reversed(FAR_FIRST):
            w_copy[k][j].wait_recv()
            f_copy[k].append(
                send(w_buf.at[k, j], w_buf.at[k, 8 + j], f_send.at[k, j], f_recv.at[k, j], sibling)
            )

    for copy in loads[2:]:
        copy.wait()

    lane = lax.broadcasted_iota(jnp.int32, (1, LT), 1)
    z_pos, y_pos = lane & 7, (lane >> 3) & 7
    low = lane < 64

    def flag(cond):
        return jnp.where(cond, 1.0, 0.0).astype(F32)

    def named(face):
        return jnp.where(near_ref[0, 0, face] >= 0, 1.0, 0.0).astype(F32)

    occupied = jnp.where(live_ref[0, 0] > 0, 1.0, 0.0).astype(F32)
    low_f, high_f = flag(low), flag(lane >= 64)
    in_z = {c: flag((z_pos + c - 1 >= 0) & (z_pos + c - 1 < 8)) for c in (0, 2)}
    in_y = {b: flag((y_pos + b - 1 >= 0) & (y_pos + b - 1 < 8)) for b in (0, 2)}

    def wide(mask):
        return jnp.broadcast_to(mask, (CH, LT)).astype(BF16)

    inside = {"low": high_f, "mid": jnp.ones((1, LT), F32), "high": low_f, "edge": jnp.zeros((1, LT), F32)}
    z_keep = {c: wide(in_z[c]) for c in (0, 2)}
    y_keep = {b: wide(in_y[b]) for b in (0, 2)}
    z_wrap = {
        (c, w): wide((1.0 - in_z[c]) * named(4 + c // 2) * inside[w]) for c in (0, 2) for w in inside
    }
    y_wrap = {}
    for b in (0, 2):
        for w in inside:
            base = (1.0 - in_y[b]) * named(2 + b // 2) * inside[w]
            for c in range(3):
                y_wrap[b, c, w] = wide(base if c == 1 else base * in_z[c])

    def unroll_tile(which, j, tile, w=None):
        w = w or ("low" if j == 0 else "high" if j == 5 else "mid")
        for c in range(3):
            if c == 1:
                along = tile
            else:
                dz = c - 1
                along = (
                    pltpu.roll(tile, -dz % LT, 1) * z_keep[c]
                    + pltpu.roll(tile, 7 * dz % LT, 1) * z_wrap[c, w]
                )
            for b in range(3):
                if b == 1:
                    both = along
                else:
                    dy = b - 1
                    both = (
                        pltpu.roll(along, -8 * dy % LT, 1) * y_keep[b]
                        + pltpu.roll(along, 56 * dy % LT, 1) * y_wrap[b, c, w]
                    )
                tap = b * 3 + c
                cols[which, tap * CH : (tap + 1) * CH, j * LT : (j + 1) * LT] = both

    halo_copy = {}

    def send_halo(which, first, last):
        halo_out[which, 0] = half_turn(first)
        halo_out[which, 1] = half_turn(last)
        halo_copy[which] = [
            send(halo_out.at[which, 0], halo_in.at[which, 0], halo_send.at[which, 0],
                 halo_recv.at[which, 0], below),
            send(halo_out.at[which, 1], halo_in.at[which, 1], halo_send.at[which, 1],
                 halo_recv.at[which, 1], above),
        ]

    def unroll_middle(which, tiles):
        cols[which, KA:KP, :] = jnp.zeros((KP - KA, 6 * LT), BF16)
        for j in range(4):
            unroll_tile(which, j + 1, tiles[j])

    def unroll_edges(which):
        for copy in halo_copy[which]:
            copy.wait_recv()
        lower = halo_out[which, 1] * wide(high_f) + halo_in[which, 1] * wide(low_f * named(0))
        unroll_tile(which, 0, lower)
        upper = halo_out[which, 0] * wide(low_f) + halo_in[which, 0] * wide(high_f * named(1))
        unroll_tile(which, 5, upper)

    def lanes_of(array, j):
        return array[:, j * LT : (j + 1) * LT]

    x_tiles = paired([feat_ref[0, 0, :, j * LT : (j + 1) * LT].astype(F32) for j in range(4)], low)
    a_one = []
    for j in range(4):
        norm, scale = normalized(x_tiles[j])
        x_buf[0, j] = x_tiles[j]
        n_buf[0, j], r_buf[0, j] = norm, scale
        a_one.append((occupied * (norm * sigmoid(norm))).astype(BF16))
    send_halo(0, a_one[0], a_one[3])
    g_tiles = paired([grad_ref[0, 0, :, j * LT : (j + 1) * LT].astype(F32) for j in range(4)], low)
    g_two = []
    for j in range(4):
        x_buf[1, j] = g_tiles[j]
        g_two.append((occupied * g_tiles[j]).astype(BF16))
    send_halo(1, g_two[0], g_two[3])
    unroll_middle(0, a_one)
    unroll_middle(1, g_two)

    r_row = lax.broadcasted_iota(jnp.int32, (LT, CH), 0)
    r_col = lax.broadcasted_iota(jnp.int32, (LT, CH), 1)
    r_core = core + (r_row >> 6) * (1 - 2 * core)
    r_owner = (((r_row >> 3) & 7) ^ chip) * 2 + r_core
    spread = jnp.where(((r_row & 7) < 6) & (r_owner * 6 + (r_row & 7) == r_col), 1.0, 0.0).astype(BF16)

    def spread_rows(tiles):
        whole_g = jnp.concatenate(list(tiles), axis=1)
        return jnp.dot(spread, whole_g, preferred_element_type=F32).astype(BF16)

    p_out = lax.broadcasted_iota(jnp.int32, (CH, 256), 0)
    p_col = lax.broadcasted_iota(jnp.int32, (CH, 256), 1)
    p_owner = (p_out * 43691) >> 18
    p_slot = ((p_owner >> 1) ^ chip) + 8 * ((p_owner & 1) ^ core)
    p_row = p_out - 6 * p_owner
    p_base = p_slot * 16 + p_row - p_col

    def picker(shift, wanted=None):
        hit = p_base + shift == 0
        return jnp.where(hit if wanted is None else hit & wanted, 1.0, 0.0).astype(BF16)

    pick_head = jnp.concatenate([picker(0), picker(6)], axis=0)
    pick_tail = picker(12, p_row < 4)
    pick_spare = jnp.concatenate([picker(8, p_row >= 4), picker(10, p_row >= 4)], axis=0)

    def assemble(k):
        for copy in f_copy[k]:
            copy.wait_recv()
        shards = w_buf[k].reshape(256, 8 * LT)
        head = jnp.dot(pick_head, shards, preferred_element_type=F32).astype(BF16)
        w_full[k, :, : 8 * LT] = head[:CH]
        w_full[k, :, 8 * LT : 16 * LT] = head[CH:]
        tail = jnp.dot(pick_tail, shards[:, : 5 * LT], preferred_element_type=F32)
        spare = jnp.dot(pick_spare, shards[:, 5 * LT :], preferred_element_type=F32)
        for n in range(5):
            top, col = CH * (n % 2), n // 2
            w_full[k, :, (16 + n) * LT : (17 + n) * LT] = (
                tail[:, n * LT : (n + 1) * LT] + spare[top : top + CH, col * LT : (col + 1) * LT]
            ).astype(BF16)

    def flip(k):
        for a in range(3):
            turned = jnp.transpose(w_full[k, :, (2 - a) * KP : (3 - a) * KP])
            blocks = [turned[(8 - t) * CH : (9 - t) * CH, :] for t in range(9)]
            w_flip[k, :, a * KP : (a + 1) * KP] = jnp.concatenate(
                blocks + [jnp.zeros((CH, KP - KA), BF16)], axis=1
            )

    def convolve(weights, k, which):
        total = None
        for a in range(3):
            part = jnp.dot(
                weights[k, :, a * KP : (a + 1) * KP],
                cols[which, :, a * LT : a * LT + 512],
                preferred_element_type=F32,
            )
            total = part if total is None else total + part
        return total

    one_copy, two_copy = {}, {}

    def first_pair(a):
        return gp_buf[...], cols[0, :, a * LT : a * LT + 512]

    def second_pair(a):
        if a == 0:
            return gp_wide[:, 2 * LT : 7 * LT], cols[2, :, LT : 6 * LT]
        if a == 1:
            return gp_wide[:, LT : 5 * LT], cols[2, :, LT : 5 * LT]
        left = jnp.concatenate([gp_wide[:, : 4 * LT], gp_wide[:, 7 * LT :]], axis=1)
        return left, cols[2, :, LT : 6 * LT]

    def start_term(m, pair):
        one_copy[m] = []
        for a in range(3):
            part = lax.dot_general(
                *pair(a),
                (((1,), (1,)), ((), ())), preferred_element_type=F32,
            )
            one_out[m, a] = part[64:].astype(BF16)
            one_copy[m].append(
                send(one_out.at[m, a], one_in.at[m, a], one_send.at[m, a], one_recv.at[m, a], sibling)
            )
            term[m, :, a * KP : (a + 1) * KP] = part[:64]

    def reduce_chips(m):
        for a in range(3):
            one_copy[m][a].wait_recv()
            term[m, :, a * KP : (a + 1) * KP] += one_in[m, a].astype(F32)
        two_copy[m] = {}
        for j in FAR_FIRST:
            two_out[m, j - 1] = packed(term[m, 8 * j : 8 * j + 6, :]).astype(BF16)
            two_copy[m][j] = send(
                two_out.at[m, j - 1], two_in.at[m, j - 1], two_send.at[m, j - 1],
                two_recv.at[m, j - 1], chip_mate(j),
            )

    def sum_chips(m):
        total = packed(term[m, :6, :])
        for j in reversed(FAR_FIRST):
            two_copy[m][j].wait_recv()
            total = total + two_in[m, j - 1].astype(F32)
        blank = jnp.zeros((2, LT), F32)
        return [jnp.concatenate([tile, blank], axis=0) for tile in unpacked(total)]

    rows_far_first = (4, 5, 3, 2, 6, 7, 1)
    later = {}

    def reduce_rows():
        other = sum_chips(1)
        both = [sum_chips(0), other]
        for p in range(7):
            joined = jnp.concatenate(
                [jnp.concatenate(tiles[3 * p : 3 * p + 3], axis=1) for tiles in both], axis=0
            )
            own_sum[p] = joined
            sum_src[p] = joined.astype(BF16)
        own_sum[7] = jnp.zeros((16, 3 * LT), F32)
        sum_src[7] = jnp.zeros((16, 3 * LT), BF16)
        later["y"] = [
            send(sum_src.at[xor(row, j)], sum_in.at[j - 1], y_send.at[j - 1], y_recv.at[j - 1], row_mate(j))
            for j in rows_far_first
        ]

    def reduce_cols():
        for copy in later["y"]:
            copy.wait_recv()
        total = own_sum[row]
        for j in range(7):
            total = total + sum_in[j].astype(F32)
        piece[...] = total.astype(BF16)
        later["z"] = [
            send(piece, piece_in.at[j - 1], z_send.at[j - 1], z_recv.at[j - 1], col_mate(j))
            for j in (2, 3, 1)
        ]

    def share_rows():
        for copy in later["z"]:
            copy.wait_recv()
        parts = [piece[...].astype(F32)] + [piece_in[j].astype(F32) for j in range(3)]
        whole[row] = ((parts[0] + parts[1]) + (parts[2] + parts[3])).astype(WHOLE)
        later["g"] = [
            send(whole.at[row], whole.at[row], g_send.at[j - 1], g_recv.at[j - 1], row_mate(j))
            for j in rows_far_first
        ]

    def finish():
        for copy in later["g"]:
            copy.wait_recv()
        pieces = [whole[p].astype(F32) for p in range(7)]
        for m, out_ref in enumerate((gone_ref, gtwo_ref)):
            flat = jnp.concatenate([one[8 * m : 8 * m + 6] for one in pieces], axis=1)
            out_ref[...] = jnp.concatenate([flat[:, a * KP : a * KP + KA] for a in range(3)], axis=1)

    def silu_tiles(hidden):
        tiles = []
        for j in range(4):
            norm, scale = normalized(lanes_of(hidden, j))
            n_buf[1, j], r_buf[1, j] = norm, scale
            tiles.append((occupied * (norm * sigmoid(norm))).astype(BF16))
        return tiles

    unroll_edges(0)
    unroll_edges(1)
    gp_wide[...] = spread_rows(
        [halo_out[1, 1] * wide(high_f)] + g_two + [halo_out[1, 0] * wide(low_f)]
        + [halo_in[1, 0] * wide(high_f * named(1)), halo_in[1, 1] * wide(low_f * named(0))]
    )
    forward_weight(0)
    forward_weight(1)
    assemble(0)
    a_two = silu_tiles(convolve(w_full, 0, 0))
    send_halo(2, a_two[0], a_two[3])
    unroll_middle(2, a_two)
    unroll_tile(2, 5, a_two[0] * wide(low_f) + a_two[3] * wide(high_f), "edge")
    start_term(1, second_pair)
    assemble(1)
    flip(1)
    back = convolve(w_flip, 1, 1)
    g_one = []
    for j in range(4):
        inner = act_vjp(n_buf[1, j], r_buf[1, j], occupied * lanes_of(back, j))
        g_one.append((occupied * inner).astype(BF16))
    send_halo(3, g_one[0], g_one[3])
    gp_buf[...] = spread_rows(g_one)
    start_term(0, first_pair)
    reduce_chips(1)
    reduce_chips(0)

    unroll_middle(3, g_one)
    flip(0)
    reduce_rows()
    unroll_edges(2)
    branch = convolve(w_full, 1, 2)
    outs = unpaired([occupied * (x_buf[0, j] + lanes_of(branch, j)) for j in range(4)], low)
    for j in range(4):
        bout_ref[0, 0, :, j * LT : (j + 1) * LT] = outs[j].astype(BF16)
    saves[0].start()
    reduce_cols()
    unroll_edges(3)
    back = convolve(w_flip, 0, 3)
    outs = []
    for j in range(4):
        inner = act_vjp(n_buf[0, j], r_buf[0, j], occupied * lanes_of(back, j))
        outs.append(occupied * (x_buf[1, j] + inner))
    outs = unpaired(outs, low)
    for j in range(4):
        gin_ref[0, 0, :, j * LT : (j + 1) * LT] = outs[j].astype(BF16)
    saves[1].start()
    share_rows()
    finish()
    saves[2].start()
    saves[3].start()
    for copy in sent:
        copy.wait_send()
    for copy in saves:
        copy.wait()


def store(*refs):
    copies = [pltpu.make_async_copy(refs[i], refs[4 + i], refs[8].at[i]) for i in range(4)]
    for copy in copies:
        copy.start()
    for copy in copies:
        copy.wait()


def body(features, w_first, w_second, neighbours, live_counts, output_gradient):
    dma = pltpu.SemaphoreType.DMA
    vmem = pl.BlockSpec(memory_space=pltpu.VMEM)
    hbm = pl.BlockSpec(memory_space=pltpu.HBM)
    results = pl.pallas_call(
        kernel,
        out_shape=(
            jax.ShapeDtypeStruct(features.shape, BF16),
            jax.ShapeDtypeStruct(features.shape, BF16),
            jax.ShapeDtypeStruct(w_first.shape, F32),
            jax.ShapeDtypeStruct(w_second.shape, F32),
        ),
        in_specs=[hbm] * 6,
        out_specs=(hbm,) * 4,
        scratch_shapes=[
            pltpu.VMEM(features.shape, BF16),
            pltpu.VMEM(features.shape, BF16),
            pltpu.VMEM(w_first.shape, F32),
            pltpu.VMEM(w_second.shape, F32),
            pltpu.VMEM(features.shape, BF16),
            pltpu.VMEM(w_first.shape, BF16),
            pltpu.VMEM(w_second.shape, BF16),
            pltpu.SMEM(neighbours.shape, jnp.int32),
            pltpu.SMEM(live_counts.shape, jnp.int32),
            pltpu.VMEM(features.shape, BF16),
            dma((6,)),
            dma((4,)),
            pltpu.VMEM((2, 16, 16, 8 * LT), BF16),
            pltpu.VMEM((2, CH, 3 * KP), BF16),
            pltpu.VMEM((2, CH, 3 * KP), BF16),
            pltpu.VMEM((4, 2, CH, LT), BF16),
            pltpu.VMEM((4, 2, CH, LT), BF16),
            pltpu.VMEM((4, KP, 6 * LT), BF16),
            pltpu.VMEM((2, 4, CH, LT), F32),
            pltpu.VMEM((2, 4, CH, LT), F32),
            pltpu.VMEM((2, 4, 1, LT), F32),
            pltpu.VMEM((LT, 512), BF16),
            pltpu.VMEM((LT, 8 * LT), BF16),
            pltpu.VMEM((2, 64, 3 * KP), F32),
            pltpu.VMEM((2, 3, 64, KP), BF16),
            pltpu.VMEM((2, 3, 64, KP), BF16),
            pltpu.VMEM((2, 7, 16, 8 * LT), BF16),
            pltpu.VMEM((2, 7, 16, 8 * LT), BF16),
            pltpu.VMEM((8, 16, 3 * LT), F32),
            pltpu.VMEM((8, 16, 3 * LT), BF16),
            pltpu.VMEM((7, 16, 3 * LT), BF16),
            pltpu.VMEM((16, 3 * LT), BF16),
            pltpu.VMEM((3, 16, 3 * LT), BF16),
            pltpu.VMEM((8, 16, 3 * LT), WHOLE),
            dma((2, 7)), dma((2, 7)), dma((2, 8)), dma((2, 8)), dma((4, 2)), dma((4, 2)),
            dma((2, 3)), dma((2, 3)), dma((2, 7)), dma((2, 7)), dma((7,)), dma((7,)),
            dma((3,)), dma((3,)), dma((7,)), dma((7,)),
        ],
        compiler_params=pltpu.CompilerParams(
            collective_id=0, has_side_effects=True, vmem_limit_bytes=63 * 1024 * 1024
        ),
    )(features, w_first, w_second, neighbours, live_counts, output_gradient)
    return pl.pallas_call(
        store,
        out_shape=tuple(jax.ShapeDtypeStruct(r.shape, r.dtype) for r in results),
        in_specs=[vmem] * 4,
        out_specs=(hbm,) * 4,
        scratch_shapes=[dma((4,))],
        compiler_params=pltpu.CompilerParams(vmem_limit_bytes=63 * 1024 * 1024),
    )(*results)


def solution(mesh):
    blocks = P("fsdp", "space", None, None)
    weights = P("fsdp", None)
    return jax.shard_map(
        body,
        mesh=mesh,
        in_specs=(blocks, weights, weights, P("fsdp", "space", None), P("fsdp", "space"), blocks),
        out_specs=(blocks, blocks, weights, weights),
        check_vma=False,
    )
```

```python
import jax
import jax.numpy as jnp
from jax import lax
from jax.experimental import pallas as pl
from jax.experimental.pallas import tpu as pltpu
from jax.sharding import PartitionSpec as P

MESH = pl.DeviceIdType.MESH
F32 = jnp.float32
BF16 = jnp.bfloat16

CH = 96
LT = 128
KA = 9 * CH
KP = 896
EPS = 1e-05
WHOLE = BF16
FAR_FIRST = (6, 2, 7, 5, 3, 1, 4)


def xor(value, pattern):
    for bit in (1, 2, 4):
        if pattern & bit:
            value = value + (1 - 2 * lax.rem(lax.div(value, bit), 2)) * bit
    return value


def half_turn(tile):
    return pltpu.roll(tile, 64, 1)


def paired(tiles, low):
    t0, t1, t2, t3 = tiles
    return (
        jnp.where(low, t0, half_turn(t2)),
        jnp.where(low, half_turn(t0), t2),
        jnp.where(low, t1, half_turn(t3)),
        jnp.where(low, half_turn(t1), t3),
    )


def unpaired(tiles, low):
    p0, p1, p2, p3 = tiles
    return (
        jnp.where(low, p0, half_turn(p1)),
        jnp.where(low, p2, half_turn(p3)),
        jnp.where(low, half_turn(p0), p1),
        jnp.where(low, half_turn(p2), p3),
    )


def packed(rows):
    tail = [rows[:, n * LT : (n + 1) * LT] for n in range(16, 21)]
    blank = jnp.zeros((2, LT), rows.dtype)
    spare = jnp.concatenate(
        [
            jnp.concatenate([tail[0][4:6], tail[2][4:6], tail[4][4:6]], axis=1),
            jnp.concatenate([tail[1][4:6], tail[3][4:6], blank], axis=1),
        ],
        axis=0,
    )
    last = jnp.concatenate([rows[:4, 16 * LT :], spare], axis=1)
    return jnp.concatenate([rows[:, : 8 * LT], rows[:, 8 * LT : 16 * LT], last], axis=0)


def unpacked(block):
    tiles = [block[:6, n * LT : (n + 1) * LT] for n in range(8)]
    tiles += [block[6:12, n * LT : (n + 1) * LT] for n in range(8)]
    for n in range(5):
        top, col = 12 + 2 * (n % 2), 5 + n // 2
        tiles.append(
            jnp.concatenate(
                [block[12:16, n * LT : (n + 1) * LT], block[top : top + 2, col * LT : (col + 1) * LT]], axis=0
            )
        )
    return tiles


def normalized(u):
    centred = u - jnp.mean(u, axis=0, keepdims=True)
    scale = lax.rsqrt(jnp.mean(centred * centred, axis=0, keepdims=True) + EPS)
    return centred * scale, scale


def sigmoid(v):
    return 1.0 / (1.0 + jnp.exp(-v))


def act_vjp(norm, scale, cotangent):
    gate = sigmoid(norm)
    inner = cotangent * (gate * (1.0 + norm * (1.0 - gate)))
    return scale * (
        inner
        - jnp.mean(inner, axis=0, keepdims=True)
        - norm * jnp.mean(inner * norm, axis=0, keepdims=True)
    )


def kernel(
    feat_hbm, wone_hbm, wtwo_hbm, near_hbm, live_hbm, grad_hbm,
    bout_hbm, gin_hbm, gone_hbm, gtwo_hbm,
    bout_ref, gin_ref, gone_ref, gtwo_ref, feat_ref, wone_ref, wtwo_ref, near_ref, live_ref, grad_ref, load_sem, save_sem,
    w_buf, w_full, w_flip, halo_out, halo_in, cols, x_buf, n_buf, r_buf, gp_buf, gp_wide,
    term, one_out, one_in, two_out, two_in, own_sum, sum_src, sum_in, piece, piece_in, whole,
    w_send, w_recv, f_send, f_recv, halo_send, halo_recv,
    one_send, one_recv, two_send, two_recv, y_send, y_recv, z_send, z_recv, g_send, g_recv,
):
    loads = [
        pltpu.make_async_copy(src, dst, load_sem.at[i])
        for i, (src, dst) in enumerate((
            (wone_hbm, wone_ref), (wtwo_hbm, wtwo_ref), (feat_hbm, feat_ref),
            (near_hbm, near_ref), (live_hbm, live_ref), (grad_hbm, grad_ref),
        ))
    ]
    for copy in loads:
        copy.start()
    fsdp = lax.axis_index("fsdp")
    space = lax.axis_index("space")
    chip, core = lax.div(fsdp, 2), lax.rem(fsdp, 2)
    row, col = lax.div(space, 4), lax.rem(space, 4)
    sibling = {"fsdp": chip * 2 + (1 - core), "space": space}

    def chip_mate(j):
        return {"fsdp": xor(chip, j) * 2 + core, "space": space}

    def row_mate(j):
        return {"fsdp": fsdp, "space": xor(row, j) * 4 + col}

    def col_mate(j):
        return {"fsdp": fsdp, "space": row * 4 + xor(col, j)}

    below = {"fsdp": fsdp, "space": lax.rem(space + 31, 32)}
    above = {"fsdp": fsdp, "space": lax.rem(space + 1, 32)}

    mates = (
        [sibling, below, above]
        + [chip_mate(j) for j in range(1, 8)]
        + [row_mate(j) for j in range(1, 8)]
        + [col_mate(j) for j in range(1, 4)]
    )
    barrier = pltpu.get_barrier_semaphore()
    for mate in mates:
        pl.semaphore_signal(barrier, inc=1, device_id=mate, device_id_type=MESH)

    sent = []

    saves = [
        pltpu.make_async_copy(src, dst, save_sem.at[i])
        for i, (src, dst) in enumerate((
            (bout_ref, bout_hbm), (gin_ref, gin_hbm), (gone_ref, gone_hbm), (gtwo_ref, gtwo_hbm),
        ))
    ]

    def send(src, dst, send_sem, recv_sem, device):
        copy = pltpu.make_async_remote_copy(
            src_ref=src, dst_ref=dst, send_sem=send_sem, recv_sem=recv_sem,
            device_id=device, device_id_type=MESH,
        )
        copy.start()
        sent.append(copy)
        return copy

    for k, ref in enumerate((wone_ref, wtwo_ref)):
        loads[k].wait()
        rows = ref[...].astype(F32)
        gap = jnp.zeros((6, KP - KA), F32)
        parts = []
        for a in range(3):
            parts += [rows[:, a * KA : (a + 1) * KA], gap]
        w_buf[k, 0] = packed(jnp.concatenate(parts, axis=1)).astype(BF16)

    pl.semaphore_wait(barrier, len(mates))

    w_copy, f_copy = [], []
    for k in range(2):
        own = [send(w_buf.at[k, 0], w_buf.at[k, 8], f_send.at[k, 0], f_recv.at[k, 0], sibling)]
        f_copy.append(own)
        w_copy.append({
            j: send(w_buf.at[k, 0], w_buf.at[k, j], w_send.at[k, j - 1], w_recv.at[k, j - 1], chip_mate(j))
            for j in FAR_FIRST
        })

    def forward_weight(k):
        for j in reversed(FAR_FIRST):
            w_copy[k][j].wait_recv()
            f_copy[k].append(
                send(w_buf.at[k, j], w_buf.at[k, 8 + j], f_send.at[k, j], f_recv.at[k, j], sibling)
            )

    for copy in loads[2:]:
        copy.wait()

    lane = lax.broadcasted_iota(jnp.int32, (1, LT), 1)
    z_pos, y_pos = lane & 7, (lane >> 3) & 7
    low = lane < 64

    def flag(cond):
        return jnp.where(cond, 1.0, 0.0).astype(F32)

    def named(face):
        return jnp.where(near_ref[0, 0, face] >= 0, 1.0, 0.0).astype(F32)

    occupied = jnp.where(live_ref[0, 0] > 0, 1.0, 0.0).astype(F32)
    low_f, high_f = flag(low), flag(lane >= 64)
    in_z = {c: flag((z_pos + c - 1 >= 0) & (z_pos + c - 1 < 8)) for c in (0, 2)}
    in_y = {b: flag((y_pos + b - 1 >= 0) & (y_pos + b - 1 < 8)) for b in (0, 2)}

    def wide(mask):
        return jnp.broadcast_to(mask, (CH, LT)).astype(BF16)

    inside = {"low": high_f, "mid": jnp.ones((1, LT), F32), "high": low_f, "edge": jnp.zeros((1, LT), F32)}
    z_keep = {c: wide(in_z[c]) for c in (0, 2)}
    y_keep = {b: wide(in_y[b]) for b in (0, 2)}
    z_wrap = {
        (c, w): wide((1.0 - in_z[c]) * named(4 + c // 2) * inside[w]) for c in (0, 2) for w in inside
    }
    y_wrap = {}
    for b in (0, 2):
        for w in inside:
            base = (1.0 - in_y[b]) * named(2 + b // 2) * inside[w]
            for c in range(3):
                y_wrap[b, c, w] = wide(base if c == 1 else base * in_z[c])

    def unroll_tile(which, j, tile, w=None):
        w = w or ("low" if j == 0 else "high" if j == 5 else "mid")
        for c in range(3):
            if c == 1:
                along = tile
            else:
                dz = c - 1
                along = (
                    pltpu.roll(tile, -dz % LT, 1) * z_keep[c]
                    + pltpu.roll(tile, 7 * dz % LT, 1) * z_wrap[c, w]
                )
            for b in range(3):
                if b == 1:
                    both = along
                else:
                    dy = b - 1
                    both = (
                        pltpu.roll(along, -8 * dy % LT, 1) * y_keep[b]
                        + pltpu.roll(along, 56 * dy % LT, 1) * y_wrap[b, c, w]
                    )
                tap = b * 3 + c
                cols[which, tap * CH : (tap + 1) * CH, j * LT : (j + 1) * LT] = both

    halo_copy = {}

    def send_halo(which, first, last):
        halo_out[which, 0] = half_turn(first)
        halo_out[which, 1] = half_turn(last)
        halo_copy[which] = [
            send(halo_out.at[which, 0], halo_in.at[which, 0], halo_send.at[which, 0],
                 halo_recv.at[which, 0], below),
            send(halo_out.at[which, 1], halo_in.at[which, 1], halo_send.at[which, 1],
                 halo_recv.at[which, 1], above),
        ]

    def unroll_middle(which, tiles):
        cols[which, KA:KP, :] = jnp.zeros((KP - KA, 6 * LT), BF16)
        for j in range(4):
            unroll_tile(which, j + 1, tiles[j])

    def unroll_edges(which):
        for copy in halo_copy[which]:
            copy.wait_recv()
        lower = halo_out[which, 1] * wide(high_f) + halo_in[which, 1] * wide(low_f * named(0))
        unroll_tile(which, 0, lower)
        upper = halo_out[which, 0] * wide(low_f) + halo_in[which, 0] * wide(high_f * named(1))
        unroll_tile(which, 5, upper)

    def lanes_of(array, j):
        return array[:, j * LT : (j + 1) * LT]

    x_tiles = paired([feat_ref[0, 0, :, j * LT : (j + 1) * LT].astype(F32) for j in range(4)], low)
    a_one = []
    for j in range(4):
        norm, scale = normalized(x_tiles[j])
        x_buf[0, j] = x_tiles[j]
        n_buf[0, j], r_buf[0, j] = norm, scale
        a_one.append((occupied * (norm * sigmoid(norm))).astype(BF16))
    send_halo(0, a_one[0], a_one[3])
    g_tiles = paired([grad_ref[0, 0, :, j * LT : (j + 1) * LT].astype(F32) for j in range(4)], low)
    g_two = []
    for j in range(4):
        x_buf[1, j] = g_tiles[j]
        g_two.append((occupied * g_tiles[j]).astype(BF16))
    send_halo(1, g_two[0], g_two[3])
    unroll_middle(0, a_one)
    unroll_middle(1, g_two)

    r_row = lax.broadcasted_iota(jnp.int32, (LT, CH), 0)
    r_col = lax.broadcasted_iota(jnp.int32, (LT, CH), 1)
    r_core = core + (r_row >> 6) * (1 - 2 * core)
    r_owner = (((r_row >> 3) & 7) ^ chip) * 2 + r_core
    spread = jnp.where(((r_row & 7) < 6) & (r_owner * 6 + (r_row & 7) == r_col), 1.0, 0.0).astype(BF16)

    def spread_rows(tiles):
        whole_g = jnp.concatenate(list(tiles), axis=1)
        return jnp.dot(spread, whole_g, preferred_element_type=F32).astype(BF16)

    p_out = lax.broadcasted_iota(jnp.int32, (CH, 256), 0)
    p_col = lax.broadcasted_iota(jnp.int32, (CH, 256), 1)
    p_owner = (p_out * 43691) >> 18
    p_slot = ((p_owner >> 1) ^ chip) + 8 * ((p_owner & 1) ^ core)
    p_row = p_out - 6 * p_owner
    p_base = p_slot * 16 + p_row - p_col

    def picker(shift, wanted=None):
        hit = p_base + shift == 0
        return jnp.where(hit if wanted is None else hit & wanted, 1.0, 0.0).astype(BF16)

    pick_head = jnp.concatenate([picker(0), picker(6)], axis=0)
    pick_tail = picker(12, p_row < 4)
    pick_spare = jnp.concatenate([picker(8, p_row >= 4), picker(10, p_row >= 4)], axis=0)

    def assemble(k):
        for copy in f_copy[k]:
            copy.wait_recv()
        shards = w_buf[k].reshape(256, 8 * LT)
        head = jnp.dot(pick_head, shards, preferred_element_type=F32).astype(BF16)
        w_full[k, :, : 8 * LT] = head[:CH]
        w_full[k, :, 8 * LT : 16 * LT] = head[CH:]
        tail = jnp.dot(pick_tail, shards[:, : 5 * LT], preferred_element_type=F32)
        spare = jnp.dot(pick_spare, shards[:, 5 * LT :], preferred_element_type=F32)
        for n in range(5):
            top, col = CH * (n % 2), n // 2
            w_full[k, :, (16 + n) * LT : (17 + n) * LT] = (
                tail[:, n * LT : (n + 1) * LT] + spare[top : top + CH, col * LT : (col + 1) * LT]
            ).astype(BF16)

    def flip(k):
        for a in range(3):
            turned = jnp.transpose(w_full[k, :, (2 - a) * KP : (3 - a) * KP])
            blocks = [turned[(8 - t) * CH : (9 - t) * CH, :] for t in range(9)]
            w_flip[k, :, a * KP : (a + 1) * KP] = jnp.concatenate(
                blocks + [jnp.zeros((CH, KP - KA), BF16)], axis=1
            )

    def convolve(weights, k, which):
        total = None
        for a in range(3):
            part = jnp.dot(
                weights[k, :, a * KP : (a + 1) * KP],
                cols[which, :, a * LT : a * LT + 512],
                preferred_element_type=F32,
            )
            total = part if total is None else total + part
        return total

    one_copy, two_copy = {}, {}

    def first_pair(a):
        return gp_buf[...], cols[0, :, a * LT : a * LT + 512]

    def second_pair(a):
        if a == 0:
            return gp_wide[:, 2 * LT : 7 * LT], cols[2, :, LT : 6 * LT]
        if a == 1:
            return gp_wide[:, LT : 5 * LT], cols[2, :, LT : 5 * LT]
        left = jnp.concatenate([gp_wide[:, : 4 * LT], gp_wide[:, 7 * LT :]], axis=1)
        return left, cols[2, :, LT : 6 * LT]

    def start_term(m, pair):
        one_copy[m] = []
        for a in range(3):
            part = lax.dot_general(
                *pair(a),
                (((1,), (1,)), ((), ())), preferred_element_type=F32,
            )
            one_out[m, a] = part[64:].astype(BF16)
            one_copy[m].append(
                send(one_out.at[m, a], one_in.at[m, a], one_send.at[m, a], one_recv.at[m, a], sibling)
            )
            term[m, :, a * KP : (a + 1) * KP] = part[:64]

    def reduce_chips(m):
        for a in range(3):
            one_copy[m][a].wait_recv()
            term[m, :, a * KP : (a + 1) * KP] += one_in[m, a].astype(F32)
        two_copy[m] = {}
        for j in FAR_FIRST:
            two_out[m, j - 1] = packed(term[m, 8 * j : 8 * j + 6, :]).astype(BF16)
            two_copy[m][j] = send(
                two_out.at[m, j - 1], two_in.at[m, j - 1], two_send.at[m, j - 1],
                two_recv.at[m, j - 1], chip_mate(j),
            )

    def sum_chips(m):
        total = packed(term[m, :6, :])
        for j in reversed(FAR_FIRST):
            two_copy[m][j].wait_recv()
            total = total + two_in[m, j - 1].astype(F32)
        return total

    rows_far_first = (4, 5, 3, 2, 6, 7, 1)
    later = {}

    def reduce_rows():
        other = sum_chips(1)
        both = [sum_chips(0), other]
        for p in range(8):
            joined = jnp.concatenate([lanes_of(block, p) for block in both], axis=0)
            own_sum[p] = joined
            sum_src[p] = joined.astype(BF16)
        later["y"] = [
            send(sum_src.at[xor(row, j)], sum_in.at[j - 1], y_send.at[j - 1], y_recv.at[j - 1], row_mate(j))
            for j in rows_far_first
        ]

    def reduce_cols():
        for copy in later["y"]:
            copy.wait_recv()
        total = own_sum[row]
        for j in range(7):
            total = total + sum_in[j].astype(F32)
        piece[...] = total.astype(BF16)
        later["z"] = [
            send(piece, piece_in.at[j - 1], z_send.at[j - 1], z_recv.at[j - 1], col_mate(j))
            for j in (2, 3, 1)
        ]

    def share_rows():
        for copy in later["z"]:
            copy.wait_recv()
        parts = [piece[...].astype(F32)] + [piece_in[j].astype(F32) for j in range(3)]
        whole[row] = ((parts[0] + parts[1]) + (parts[2] + parts[3])).astype(WHOLE)
        later["g"] = [
            send(whole.at[row], whole.at[row], g_send.at[j - 1], g_recv.at[j - 1], row_mate(j))
            for j in rows_far_first
        ]

    def finish():
        for copy in later["g"]:
            copy.wait_recv()
        for m, out_ref in enumerate((gone_ref, gtwo_ref)):
            block = jnp.concatenate(
                [whole[p, 16 * m : 16 * m + 16, :].astype(F32) for p in range(8)], axis=1
            )
            flat = jnp.concatenate(unpacked(block), axis=1)
            out_ref[...] = jnp.concatenate([flat[:, a * KP : a * KP + KA] for a in range(3)], axis=1)

    def silu_tiles(hidden):
        tiles = []
        for j in range(4):
            norm, scale = normalized(lanes_of(hidden, j))
            n_buf[1, j], r_buf[1, j] = norm, scale
            tiles.append((occupied * (norm * sigmoid(norm))).astype(BF16))
        return tiles

    unroll_edges(0)
    unroll_edges(1)
    gp_wide[...] = spread_rows(
        [halo_out[1, 1] * wide(high_f)] + g_two + [halo_out[1, 0] * wide(low_f)]
        + [halo_in[1, 0] * wide(high_f * named(1)), halo_in[1, 1] * wide(low_f * named(0))]
    )
    forward_weight(0)
    forward_weight(1)
    assemble(0)
    a_two = silu_tiles(convolve(w_full, 0, 0))
    send_halo(2, a_two[0], a_two[3])
    unroll_middle(2, a_two)
    unroll_tile(2, 5, a_two[0] * wide(low_f) + a_two[3] * wide(high_f), "edge")
    start_term(1, second_pair)
    assemble(1)
    flip(1)
    back = convolve(w_flip, 1, 1)
    g_one = []
    for j in range(4):
        inner = act_vjp(n_buf[1, j], r_buf[1, j], occupied * lanes_of(back, j))
        g_one.append((occupied * inner).astype(BF16))
    send_halo(3, g_one[0], g_one[3])
    reduce_chips(1)
    gp_buf[...] = spread_rows(g_one)
    start_term(0, first_pair)
    reduce_chips(0)

    unroll_middle(3, g_one)
    flip(0)
    reduce_rows()
    unroll_edges(2)
    branch = convolve(w_full, 1, 2)
    outs = unpaired([occupied * (x_buf[0, j] + lanes_of(branch, j)) for j in range(4)], low)
    for j in range(4):
        bout_ref[0, 0, :, j * LT : (j + 1) * LT] = outs[j].astype(BF16)
    saves[0].start()
    reduce_cols()
    unroll_edges(3)
    back = convolve(w_flip, 0, 3)
    outs = []
    for j in range(4):
        inner = act_vjp(n_buf[0, j], r_buf[0, j], occupied * lanes_of(back, j))
        outs.append(occupied * (x_buf[1, j] + inner))
    outs = unpaired(outs, low)
    for j in range(4):
        gin_ref[0, 0, :, j * LT : (j + 1) * LT] = outs[j].astype(BF16)
    saves[1].start()
    share_rows()
    finish()
    saves[2].start()
    saves[3].start()
    for copy in sent:
        copy.wait_send()
    for copy in saves:
        copy.wait()


def store(*refs):
    copies = [pltpu.make_async_copy(refs[i], refs[4 + i], refs[8].at[i]) for i in range(4)]
    for copy in copies:
        copy.start()
    for copy in copies:
        copy.wait()


def body(features, w_first, w_second, neighbours, live_counts, output_gradient):
    dma = pltpu.SemaphoreType.DMA
    vmem = pl.BlockSpec(memory_space=pltpu.VMEM)
    hbm = pl.BlockSpec(memory_space=pltpu.HBM)
    results = pl.pallas_call(
        kernel,
        out_shape=(
            jax.ShapeDtypeStruct(features.shape, BF16),
            jax.ShapeDtypeStruct(features.shape, BF16),
            jax.ShapeDtypeStruct(w_first.shape, F32),
            jax.ShapeDtypeStruct(w_second.shape, F32),
        ),
        in_specs=[hbm] * 6,
        out_specs=(hbm,) * 4,
        scratch_shapes=[
            pltpu.VMEM(features.shape, BF16),
            pltpu.VMEM(features.shape, BF16),
            pltpu.VMEM(w_first.shape, F32),
            pltpu.VMEM(w_second.shape, F32),
            pltpu.VMEM(features.shape, BF16),
            pltpu.VMEM(w_first.shape, BF16),
            pltpu.VMEM(w_second.shape, BF16),
            pltpu.SMEM(neighbours.shape, jnp.int32),
            pltpu.SMEM(live_counts.shape, jnp.int32),
            pltpu.VMEM(features.shape, BF16),
            dma((6,)),
            dma((4,)),
            pltpu.VMEM((2, 16, 16, 8 * LT), BF16),
            pltpu.VMEM((2, CH, 3 * KP), BF16),
            pltpu.VMEM((2, CH, 3 * KP), BF16),
            pltpu.VMEM((4, 2, CH, LT), BF16),
            pltpu.VMEM((4, 2, CH, LT), BF16),
            pltpu.VMEM((4, KP, 6 * LT), BF16),
            pltpu.VMEM((2, 4, CH, LT), F32),
            pltpu.VMEM((2, 4, CH, LT), F32),
            pltpu.VMEM((2, 4, 1, LT), F32),
            pltpu.VMEM((LT, 512), BF16),
            pltpu.VMEM((LT, 8 * LT), BF16),
            pltpu.VMEM((2, 64, 3 * KP), F32),
            pltpu.VMEM((2, 3, 64, KP), BF16),
            pltpu.VMEM((2, 3, 64, KP), BF16),
            pltpu.VMEM((2, 7, 16, 8 * LT), BF16),
            pltpu.VMEM((2, 7, 16, 8 * LT), BF16),
            pltpu.VMEM((8, 32, LT), F32),
            pltpu.VMEM((8, 32, LT), BF16),
            pltpu.VMEM((7, 32, LT), BF16),
            pltpu.VMEM((32, LT), BF16),
            pltpu.VMEM((3, 32, LT), BF16),
            pltpu.VMEM((8, 32, LT), WHOLE),
            dma((2, 7)), dma((2, 7)), dma((2, 8)), dma((2, 8)), dma((4, 2)), dma((4, 2)),
            dma((2, 3)), dma((2, 3)), dma((2, 7)), dma((2, 7)), dma((7,)), dma((7,)),
            dma((3,)), dma((3,)), dma((7,)), dma((7,)),
        ],
        compiler_params=pltpu.CompilerParams(
            collective_id=0, has_side_effects=True, vmem_limit_bytes=63 * 1024 * 1024
        ),
    )(features, w_first, w_second, neighbours, live_counts, output_gradient)
    return pl.pallas_call(
        store,
        out_shape=tuple(jax.ShapeDtypeStruct(r.shape, r.dtype) for r in results),
        in_specs=[vmem] * 4,
        out_specs=(hbm,) * 4,
        scratch_shapes=[dma((4,))],
        compiler_params=pltpu.CompilerParams(vmem_limit_bytes=63 * 1024 * 1024),
    )(*results)


def solution(mesh):
    blocks = P("fsdp", "space", None, None)
    weights = P("fsdp", None)
    return jax.shard_map(
        body,
        mesh=mesh,
        in_specs=(blocks, weights, weights, P("fsdp", "space", None), P("fsdp", "space"), blocks),
        out_specs=(blocks, blocks, weights, weights),
        check_vma=False,
    )
```

```python
import jax
import jax.numpy as jnp
from jax import lax
from jax.experimental import pallas as pl
from jax.experimental.pallas import tpu as pltpu
from jax.sharding import PartitionSpec as P

MESH = pl.DeviceIdType.MESH
F32 = jnp.float32
BF16 = jnp.bfloat16

CH = 96
LT = 128
KA = 9 * CH
KP = 896
EPS = 1e-05
WHOLE = BF16
FAR_FIRST = (6, 2, 7, 5, 3, 1, 4)


def xor(value, pattern):
    for bit in (1, 2, 4):
        if pattern & bit:
            value = value + (1 - 2 * lax.rem(lax.div(value, bit), 2)) * bit
    return value


def half_turn(tile):
    return pltpu.roll(tile, 64, 1)


def paired(tiles, low):
    t0, t1, t2, t3 = tiles
    return (
        jnp.where(low, t0, half_turn(t2)),
        jnp.where(low, half_turn(t0), t2),
        jnp.where(low, t1, half_turn(t3)),
        jnp.where(low, half_turn(t1), t3),
    )


def unpaired(tiles, low):
    p0, p1, p2, p3 = tiles
    return (
        jnp.where(low, p0, half_turn(p1)),
        jnp.where(low, p2, half_turn(p3)),
        jnp.where(low, half_turn(p0), p1),
        jnp.where(low, half_turn(p2), p3),
    )


def packed(rows):
    tail = [rows[:, n * LT : (n + 1) * LT] for n in range(16, 21)]
    blank = jnp.zeros((2, LT), rows.dtype)
    spare = jnp.concatenate(
        [
            jnp.concatenate([tail[0][4:6], tail[2][4:6], tail[4][4:6]], axis=1),
            jnp.concatenate([tail[1][4:6], tail[3][4:6], blank], axis=1),
        ],
        axis=0,
    )
    last = jnp.concatenate([rows[:4, 16 * LT :], spare], axis=1)
    return jnp.concatenate([rows[:, : 8 * LT], rows[:, 8 * LT : 16 * LT], last], axis=0)


def unpacked(block):
    tiles = [block[:6, n * LT : (n + 1) * LT] for n in range(8)]
    tiles += [block[6:12, n * LT : (n + 1) * LT] for n in range(8)]
    for n in range(5):
        top, col = 12 + 2 * (n % 2), 5 + n // 2
        tiles.append(
            jnp.concatenate(
                [block[12:16, n * LT : (n + 1) * LT], block[top : top + 2, col * LT : (col + 1) * LT]], axis=0
            )
        )
    return tiles


def normalized(u):
    centred = u - jnp.mean(u, axis=0, keepdims=True)
    scale = lax.rsqrt(jnp.mean(centred * centred, axis=0, keepdims=True) + EPS)
    return centred * scale, scale


def sigmoid(v):
    return 1.0 / (1.0 + jnp.exp(-v))


def act_vjp(norm, scale, cotangent):
    gate = sigmoid(norm)
    inner = cotangent * (gate * (1.0 + norm * (1.0 - gate)))
    return scale * (
        inner
        - jnp.mean(inner, axis=0, keepdims=True)
        - norm * jnp.mean(inner * norm, axis=0, keepdims=True)
    )


def kernel(
    feat_hbm, wone_hbm, wtwo_hbm, near_hbm, live_hbm, grad_hbm,
    bout_hbm, gin_hbm, gone_hbm, gtwo_hbm,
    bout_ref, gin_ref, gone_ref, gtwo_ref, feat_ref, wone_ref, wtwo_ref, near_ref, live_ref, grad_ref, load_sem, save_sem,
    w_buf, w_full, w_flip, halo_out, halo_in, cols, x_buf, n_buf, r_buf, gp_buf, gp_wide,
    term, one_out, one_in, two_out, two_in, own_sum, sum_src, sum_in, piece, piece_in, whole,
    w_send, w_recv, f_send, f_recv, halo_send, halo_recv,
    one_send, one_recv, two_send, two_recv, y_send, y_recv, z_send, z_recv, g_send, g_recv,
):
    loads = [
        pltpu.make_async_copy(src, dst, load_sem.at[i])
        for i, (src, dst) in enumerate((
            (wone_hbm, wone_ref), (wtwo_hbm, wtwo_ref), (feat_hbm, feat_ref),
            (near_hbm, near_ref), (live_hbm, live_ref), (grad_hbm, grad_ref),
        ))
    ]
    for copy in loads:
        copy.start()
    fsdp = lax.axis_index("fsdp")
    space = lax.axis_index("space")
    chip, core = lax.div(fsdp, 2), lax.rem(fsdp, 2)
    row, col = lax.div(space, 4), lax.rem(space, 4)
    sibling = {"fsdp": chip * 2 + (1 - core), "space": space}

    def chip_mate(j):
        return {"fsdp": xor(chip, j) * 2 + core, "space": space}

    def row_mate(j):
        return {"fsdp": fsdp, "space": xor(row, j) * 4 + col}

    def col_mate(j):
        return {"fsdp": fsdp, "space": row * 4 + xor(col, j)}

    below = {"fsdp": fsdp, "space": lax.rem(space + 31, 32)}
    above = {"fsdp": fsdp, "space": lax.rem(space + 1, 32)}

    mates = (
        [sibling, below, above]
        + [chip_mate(j) for j in range(1, 8)]
        + [row_mate(j) for j in range(1, 8)]
        + [col_mate(j) for j in range(1, 4)]
    )
    barrier = pltpu.get_barrier_semaphore()
    for mate in mates:
        pl.semaphore_signal(barrier, inc=1, device_id=mate, device_id_type=MESH)

    sent = []

    saves = [
        pltpu.make_async_copy(src, dst, save_sem.at[i])
        for i, (src, dst) in enumerate((
            (bout_ref, bout_hbm), (gin_ref, gin_hbm), (gone_ref, gone_hbm), (gtwo_ref, gtwo_hbm),
        ))
    ]

    def send(src, dst, send_sem, recv_sem, device):
        copy = pltpu.make_async_remote_copy(
            src_ref=src, dst_ref=dst, send_sem=send_sem, recv_sem=recv_sem,
            device_id=device, device_id_type=MESH,
        )
        copy.start()
        sent.append(copy)
        return copy

    def pack_weight(k, ref):
        loads[k].wait()
        rows = ref[...].astype(F32)
        gap = jnp.zeros((6, KP - KA), F32)
        parts = []
        for a in range(3):
            parts += [rows[:, a * KA : (a + 1) * KA], gap]
        w_buf[k, 0] = packed(jnp.concatenate(parts, axis=1)).astype(BF16)

    pack_weight(0, wone_ref)
    pl.semaphore_wait(barrier, len(mates))

    w_copy, f_copy = [], []
    for k in range(2):
        if k == 1:
            pack_weight(1, wtwo_ref)
        own = [send(w_buf.at[k, 0], w_buf.at[k, 8], f_send.at[k, 0], f_recv.at[k, 0], sibling)]
        f_copy.append(own)
        w_copy.append({
            j: send(w_buf.at[k, 0], w_buf.at[k, j], w_send.at[k, j - 1], w_recv.at[k, j - 1], chip_mate(j))
            for j in FAR_FIRST
        })

    def forward_weight(k):
        for j in reversed(FAR_FIRST):
            w_copy[k][j].wait_recv()
            f_copy[k].append(
                send(w_buf.at[k, j], w_buf.at[k, 8 + j], f_send.at[k, j], f_recv.at[k, j], sibling)
            )

    for copy in loads[2:]:
        copy.wait()

    lane = lax.broadcasted_iota(jnp.int32, (1, LT), 1)
    z_pos, y_pos = lane & 7, (lane >> 3) & 7
    low = lane < 64

    def flag(cond):
        return jnp.where(cond, 1.0, 0.0).astype(F32)

    def named(face):
        return jnp.where(near_ref[0, 0, face] >= 0, 1.0, 0.0).astype(F32)

    occupied = jnp.where(live_ref[0, 0] > 0, 1.0, 0.0).astype(F32)
    low_f, high_f = flag(low), flag(lane >= 64)
    in_z = {c: flag((z_pos + c - 1 >= 0) & (z_pos + c - 1 < 8)) for c in (0, 2)}
    in_y = {b: flag((y_pos + b - 1 >= 0) & (y_pos + b - 1 < 8)) for b in (0, 2)}

    def wide(mask):
        return jnp.broadcast_to(mask, (CH, LT)).astype(BF16)

    inside = {"low": high_f, "mid": jnp.ones((1, LT), F32), "high": low_f, "edge": jnp.zeros((1, LT), F32)}
    z_keep = {c: wide(in_z[c]) for c in (0, 2)}
    y_keep = {b: wide(in_y[b]) for b in (0, 2)}
    z_wrap = {
        (c, w): wide((1.0 - in_z[c]) * named(4 + c // 2) * inside[w]) for c in (0, 2) for w in inside
    }
    y_wrap = {}
    for b in (0, 2):
        for w in inside:
            base = (1.0 - in_y[b]) * named(2 + b // 2) * inside[w]
            for c in range(3):
                y_wrap[b, c, w] = wide(base if c == 1 else base * in_z[c])

    def unroll_tile(which, j, tile, w=None):
        w = w or ("low" if j == 0 else "high" if j == 5 else "mid")
        for c in range(3):
            if c == 1:
                along = tile
            else:
                dz = c - 1
                along = (
                    pltpu.roll(tile, -dz % LT, 1) * z_keep[c]
                    + pltpu.roll(tile, 7 * dz % LT, 1) * z_wrap[c, w]
                )
            for b in range(3):
                if b == 1:
                    both = along
                else:
                    dy = b - 1
                    both = (
                        pltpu.roll(along, -8 * dy % LT, 1) * y_keep[b]
                        + pltpu.roll(along, 56 * dy % LT, 1) * y_wrap[b, c, w]
                    )
                tap = b * 3 + c
                cols[which, tap * CH : (tap + 1) * CH, j * LT : (j + 1) * LT] = both

    halo_copy = {}

    def send_halo(which, first, last):
        halo_out[which, 0] = half_turn(first)
        halo_out[which, 1] = half_turn(last)
        halo_copy[which] = [
            send(halo_out.at[which, 0], halo_in.at[which, 0], halo_send.at[which, 0],
                 halo_recv.at[which, 0], below),
            send(halo_out.at[which, 1], halo_in.at[which, 1], halo_send.at[which, 1],
                 halo_recv.at[which, 1], above),
        ]

    def unroll_middle(which, tiles):
        cols[which, KA:KP, :] = jnp.zeros((KP - KA, 6 * LT), BF16)
        for j in range(4):
            unroll_tile(which, j + 1, tiles[j])

    def unroll_edges(which):
        for copy in halo_copy[which]:
            copy.wait_recv()
        lower = halo_out[which, 1] * wide(high_f) + halo_in[which, 1] * wide(low_f * named(0))
        unroll_tile(which, 0, lower)
        upper = halo_out[which, 0] * wide(low_f) + halo_in[which, 0] * wide(high_f * named(1))
        unroll_tile(which, 5, upper)

    def lanes_of(array, j):
        return array[:, j * LT : (j + 1) * LT]

    x_tiles = paired([feat_ref[0, 0, :, j * LT : (j + 1) * LT].astype(F32) for j in range(4)], low)
    a_one = []
    for j in range(4):
        norm, scale = normalized(x_tiles[j])
        x_buf[0, j] = x_tiles[j]
        n_buf[0, j], r_buf[0, j] = norm, scale
        a_one.append((occupied * (norm * sigmoid(norm))).astype(BF16))
    send_halo(0, a_one[0], a_one[3])
    g_tiles = paired([grad_ref[0, 0, :, j * LT : (j + 1) * LT].astype(F32) for j in range(4)], low)
    g_two = []
    for j in range(4):
        x_buf[1, j] = g_tiles[j]
        g_two.append((occupied * g_tiles[j]).astype(BF16))
    send_halo(1, g_two[0], g_two[3])
    unroll_middle(0, a_one)
    unroll_middle(1, g_two)

    r_row = lax.broadcasted_iota(jnp.int32, (LT, CH), 0)
    r_col = lax.broadcasted_iota(jnp.int32, (LT, CH), 1)
    r_core = core + (r_row >> 6) * (1 - 2 * core)
    r_owner = (((r_row >> 3) & 7) ^ chip) * 2 + r_core
    spread = jnp.where(((r_row & 7) < 6) & (r_owner * 6 + (r_row & 7) == r_col), 1.0, 0.0).astype(BF16)

    def spread_rows(tiles):
        whole_g = jnp.concatenate(list(tiles), axis=1)
        return jnp.dot(spread, whole_g, preferred_element_type=F32).astype(BF16)

    p_out = lax.broadcasted_iota(jnp.int32, (CH, 256), 0)
    p_col = lax.broadcasted_iota(jnp.int32, (CH, 256), 1)
    p_owner = (p_out * 43691) >> 18
    p_slot = ((p_owner >> 1) ^ chip) + 8 * ((p_owner & 1) ^ core)
    p_row = p_out - 6 * p_owner
    p_base = p_slot * 16 + p_row - p_col

    def picker(shift, wanted=None):
        hit = p_base + shift == 0
        return jnp.where(hit if wanted is None else hit & wanted, 1.0, 0.0).astype(BF16)

    pick_head = jnp.concatenate([picker(0), picker(6)], axis=0)
    pick_tail = picker(12, p_row < 4)
    pick_spare = jnp.concatenate([picker(8, p_row >= 4), picker(10, p_row >= 4)], axis=0)

    def assemble(k):
        for copy in f_copy[k]:
            copy.wait_recv()
        shards = w_buf[k].reshape(256, 8 * LT)
        head = jnp.dot(pick_head, shards, preferred_element_type=F32).astype(BF16)
        w_full[k, :, : 8 * LT] = head[:CH]
        w_full[k, :, 8 * LT : 16 * LT] = head[CH:]
        tail = jnp.dot(pick_tail, shards[:, : 5 * LT], preferred_element_type=F32)
        spare = jnp.dot(pick_spare, shards[:, 5 * LT :], preferred_element_type=F32)
        for n in range(5):
            top, col = CH * (n % 2), n // 2
            w_full[k, :, (16 + n) * LT : (17 + n) * LT] = (
                tail[:, n * LT : (n + 1) * LT] + spare[top : top + CH, col * LT : (col + 1) * LT]
            ).astype(BF16)

    def flip(k):
        for a in range(3):
            turned = jnp.transpose(w_full[k, :, (2 - a) * KP : (3 - a) * KP])
            blocks = [turned[(8 - t) * CH : (9 - t) * CH, :] for t in range(9)]
            w_flip[k, :, a * KP : (a + 1) * KP] = jnp.concatenate(
                blocks + [jnp.zeros((CH, KP - KA), BF16)], axis=1
            )

    def convolve(weights, k, which):
        total = None
        for a in range(3):
            part = jnp.dot(
                weights[k, :, a * KP : (a + 1) * KP],
                cols[which, :, a * LT : a * LT + 512],
                preferred_element_type=F32,
            )
            total = part if total is None else total + part
        return total

    one_copy, two_copy = {}, {}

    def first_pair(a):
        return gp_buf[...], cols[0, :, a * LT : a * LT + 512]

    def second_pair(a):
        if a == 0:
            return gp_wide[:, 2 * LT : 7 * LT], cols[2, :, LT : 6 * LT]
        if a == 1:
            return gp_wide[:, LT : 5 * LT], cols[2, :, LT : 5 * LT]
        left = jnp.concatenate([gp_wide[:, : 4 * LT], gp_wide[:, 7 * LT :]], axis=1)
        return left, cols[2, :, LT : 6 * LT]

    def start_term(m, pair):
        one_copy[m] = []
        for a in range(3):
            part = lax.dot_general(
                *pair(a),
                (((1,), (1,)), ((), ())), preferred_element_type=F32,
            )
            one_out[m, a] = part[64:].astype(BF16)
            one_copy[m].append(
                send(one_out.at[m, a], one_in.at[m, a], one_send.at[m, a], one_recv.at[m, a], sibling)
            )
            term[m, :, a * KP : (a + 1) * KP] = part[:64]

    def reduce_chips(m):
        for a in range(3):
            one_copy[m][a].wait_recv()
            term[m, :, a * KP : (a + 1) * KP] += one_in[m, a].astype(F32)
        two_copy[m] = {}
        for j in FAR_FIRST:
            two_out[m, j - 1] = packed(term[m, 8 * j : 8 * j + 6, :]).astype(BF16)
            two_copy[m][j] = send(
                two_out.at[m, j - 1], two_in.at[m, j - 1], two_send.at[m, j - 1],
                two_recv.at[m, j - 1], chip_mate(j),
            )

    def sum_chips(m):
        total = packed(term[m, :6, :])
        for j in reversed(FAR_FIRST):
            two_copy[m][j].wait_recv()
            total = total + two_in[m, j - 1].astype(F32)
        return total

    rows_far_first = (4, 5, 3, 2, 6, 7, 1)
    later = {}

    def reduce_rows():
        other = sum_chips(1)
        both = [sum_chips(0), other]
        for p in range(8):
            joined = jnp.concatenate([lanes_of(block, p) for block in both], axis=0)
            own_sum[p] = joined
            sum_src[p] = joined.astype(BF16)
        later["y"] = [
            send(sum_src.at[xor(row, j)], sum_in.at[j - 1], y_send.at[j - 1], y_recv.at[j - 1], row_mate(j))
            for j in rows_far_first
        ]

    def reduce_cols():
        for copy in later["y"]:
            copy.wait_recv()
        total = own_sum[row]
        for j in range(7):
            total = total + sum_in[j].astype(F32)
        piece[...] = total.astype(BF16)
        later["z"] = [
            send(piece, piece_in.at[j - 1], z_send.at[j - 1], z_recv.at[j - 1], col_mate(j))
            for j in (2, 3, 1)
        ]

    def share_rows():
        for copy in later["z"]:
            copy.wait_recv()
        parts = [piece[...].astype(F32)] + [piece_in[j].astype(F32) for j in range(3)]
        whole[row] = ((parts[0] + parts[1]) + (parts[2] + parts[3])).astype(WHOLE)
        later["g"] = [
            send(whole.at[row], whole.at[row], g_send.at[j - 1], g_recv.at[j - 1], row_mate(j))
            for j in rows_far_first
        ]

    def finish():
        for copy in later["g"]:
            copy.wait_recv()
        for m, out_ref in enumerate((gone_ref, gtwo_ref)):
            block = jnp.concatenate(
                [whole[p, 16 * m : 16 * m + 16, :].astype(F32) for p in range(8)], axis=1
            )
            flat = jnp.concatenate(unpacked(block), axis=1)
            out_ref[...] = jnp.concatenate([flat[:, a * KP : a * KP + KA] for a in range(3)], axis=1)

    def silu_tiles(hidden):
        tiles = []
        for j in range(4):
            norm, scale = normalized(lanes_of(hidden, j))
            n_buf[1, j], r_buf[1, j] = norm, scale
            tiles.append((occupied * (norm * sigmoid(norm))).astype(BF16))
        return tiles

    unroll_edges(0)
    unroll_edges(1)
    gp_wide[...] = spread_rows(
        [halo_out[1, 1] * wide(high_f)] + g_two + [halo_out[1, 0] * wide(low_f)]
        + [halo_in[1, 0] * wide(high_f * named(1)), halo_in[1, 1] * wide(low_f * named(0))]
    )
    forward_weight(0)
    forward_weight(1)
    assemble(0)
    a_two = silu_tiles(convolve(w_full, 0, 0))
    send_halo(2, a_two[0], a_two[3])
    unroll_middle(2, a_two)
    unroll_tile(2, 5, a_two[0] * wide(low_f) + a_two[3] * wide(high_f), "edge")
    start_term(1, second_pair)
    assemble(1)
    flip(1)
    back = convolve(w_flip, 1, 1)
    g_one = []
    for j in range(4):
        inner = act_vjp(n_buf[1, j], r_buf[1, j], occupied * lanes_of(back, j))
        g_one.append((occupied * inner).astype(BF16))
    send_halo(3, g_one[0], g_one[3])
    reduce_chips(1)
    gp_buf[...] = spread_rows(g_one)
    start_term(0, first_pair)
    reduce_chips(0)

    unroll_middle(3, g_one)
    flip(0)
    reduce_rows()
    unroll_edges(2)
    branch = convolve(w_full, 1, 2)
    outs = unpaired([occupied * (x_buf[0, j] + lanes_of(branch, j)) for j in range(4)], low)
    for j in range(4):
        bout_ref[0, 0, :, j * LT : (j + 1) * LT] = outs[j].astype(BF16)
    saves[0].start()
    reduce_cols()
    unroll_edges(3)
    back = convolve(w_flip, 0, 3)
    outs = []
    for j in range(4):
        inner = act_vjp(n_buf[0, j], r_buf[0, j], occupied * lanes_of(back, j))
        outs.append(occupied * (x_buf[1, j] + inner))
    outs = unpaired(outs, low)
    for j in range(4):
        gin_ref[0, 0, :, j * LT : (j + 1) * LT] = outs[j].astype(BF16)
    saves[1].start()
    share_rows()
    finish()
    saves[2].start()
    saves[3].start()
    for copy in sent:
        copy.wait_send()
    for copy in saves:
        copy.wait()


def store(*refs):
    copies = [pltpu.make_async_copy(refs[i], refs[4 + i], refs[8].at[i]) for i in range(4)]
    for copy in copies:
        copy.start()
    for copy in copies:
        copy.wait()


def body(features, w_first, w_second, neighbours, live_counts, output_gradient):
    dma = pltpu.SemaphoreType.DMA
    vmem = pl.BlockSpec(memory_space=pltpu.VMEM)
    hbm = pl.BlockSpec(memory_space=pltpu.HBM)
    results = pl.pallas_call(
        kernel,
        out_shape=(
            jax.ShapeDtypeStruct(features.shape, BF16),
            jax.ShapeDtypeStruct(features.shape, BF16),
            jax.ShapeDtypeStruct(w_first.shape, F32),
            jax.ShapeDtypeStruct(w_second.shape, F32),
        ),
        in_specs=[hbm] * 6,
        out_specs=(hbm,) * 4,
        scratch_shapes=[
            pltpu.VMEM(features.shape, BF16),
            pltpu.VMEM(features.shape, BF16),
            pltpu.VMEM(w_first.shape, F32),
            pltpu.VMEM(w_second.shape, F32),
            pltpu.VMEM(features.shape, BF16),
            pltpu.VMEM(w_first.shape, BF16),
            pltpu.VMEM(w_second.shape, BF16),
            pltpu.SMEM(neighbours.shape, jnp.int32),
            pltpu.SMEM(live_counts.shape, jnp.int32),
            pltpu.VMEM(features.shape, BF16),
            dma((6,)),
            dma((4,)),
            pltpu.VMEM((2, 16, 16, 8 * LT), BF16),
            pltpu.VMEM((2, CH, 3 * KP), BF16),
            pltpu.VMEM((2, CH, 3 * KP), BF16),
            pltpu.VMEM((4, 2, CH, LT), BF16),
            pltpu.VMEM((4, 2, CH, LT), BF16),
            pltpu.VMEM((4, KP, 6 * LT), BF16),
            pltpu.VMEM((2, 4, CH, LT), F32),
            pltpu.VMEM((2, 4, CH, LT), F32),
            pltpu.VMEM((2, 4, 1, LT), F32),
            pltpu.VMEM((LT, 512), BF16),
            pltpu.VMEM((LT, 8 * LT), BF16),
            pltpu.VMEM((2, 64, 3 * KP), F32),
            pltpu.VMEM((2, 3, 64, KP), BF16),
            pltpu.VMEM((2, 3, 64, KP), BF16),
            pltpu.VMEM((2, 7, 16, 8 * LT), BF16),
            pltpu.VMEM((2, 7, 16, 8 * LT), BF16),
            pltpu.VMEM((8, 32, LT), F32),
            pltpu.VMEM((8, 32, LT), BF16),
            pltpu.VMEM((7, 32, LT), BF16),
            pltpu.VMEM((32, LT), BF16),
            pltpu.VMEM((3, 32, LT), BF16),
            pltpu.VMEM((8, 32, LT), WHOLE),
            dma((2, 7)), dma((2, 7)), dma((2, 8)), dma((2, 8)), dma((4, 2)), dma((4, 2)),
            dma((2, 3)), dma((2, 3)), dma((2, 7)), dma((2, 7)), dma((7,)), dma((7,)),
            dma((3,)), dma((3,)), dma((7,)), dma((7,)),
        ],
        compiler_params=pltpu.CompilerParams(
            collective_id=0, has_side_effects=True, vmem_limit_bytes=63 * 1024 * 1024
        ),
    )(features, w_first, w_second, neighbours, live_counts, output_gradient)
    return pl.pallas_call(
        store,
        out_shape=tuple(jax.ShapeDtypeStruct(r.shape, r.dtype) for r in results),
        in_specs=[vmem] * 4,
        out_specs=(hbm,) * 4,
        scratch_shapes=[dma((4,))],
        compiler_params=pltpu.CompilerParams(vmem_limit_bytes=63 * 1024 * 1024),
    )(*results)


def solution(mesh):
    blocks = P("fsdp", "space", None, None)
    weights = P("fsdp", None)
    return jax.shard_map(
        body,
        mesh=mesh,
        in_specs=(blocks, weights, weights, P("fsdp", "space", None), P("fsdp", "space"), blocks),
        out_specs=(blocks, blocks, weights, weights),
        check_vma=False,
    )
```
